128 devices in a mesh: row: 8 (over z, x_hi), col: 16 (over x_lo, y, core).
Axes of the slice: x: 4 (x_hi: 2, x_lo: 2; x = x_hi * 2 + x_lo), y: 4, z: 4, core: 2. Of those that a mesh axis runs over, the one named last changes fastest.
Arguments:
- tokens: bfloat16 [4096, 3584], P(('row', 'col')), may hold values from -24 to 24
- cotangent: bfloat16 [4096, 3584], P(('row', 'col')), may hold values from -6 to 6
- router: bfloat16 [3584, 128], replicated, may hold values from -0.09375 to 0.09375
- picks: int32 [4096, 8], P(('row', 'col')), may hold values from 0 to 127, all different within a row; in each aligned block of 32 rows (0 to 31, 32 to 63, ...) at most 3 rows name the same one
- language: int32 [4096], P(('row', 'col')), may hold values from 0 to 7
- teacher: float32 [8, 128], replicated, may hold values from 0.02 to 0.98
- w_gate: bfloat16 [128, 3584, 1024], P(('row', 'col')), may hold values from -0.09375 to 0.09375
- w_up: bfloat16 [128, 3584, 1024], P(('row', 'col')), may hold values from -0.09375 to 0.09375
- w_down: bfloat16 [128, 1024, 3584], P(('row', 'col')), may hold values from -0.1875 to 0.1875
Outputs:
- token_grad: bfloat16 [4096, 3584], P(('row', 'col'))
- router_grad: float32 [3584, 128], P(('row', 'col'))
The draws below stay inside these ranges and needn't reach their ends.
Inputs may be any that keep to these rules, and one draw needn't show every extreme that they name: `picks`: each token names 8 different experts. Within the rows of one device (aligned blocks of 32 tokens) no expert is named by more than 3 tokens, a bound that some block reaches.
All inputs are finite; a program needn't handle non-finite values.
Results may differ from the reference program's by a relative error of at most 0.007.
Values may be sent and summed in bfloat16 or wider, within the bound.
A program may use at most 128 MiB of HBM per device.

```python
import math
import jax
import jax.numpy as jnp
import numpy as np
from jax import lax

D = 3584
FF = 1024
TOP = 8
LANGS = 8
TOK_DEV = 32
EXPERTS = 128
TOKENS = 4096
CAP = 3
DEVICES = 128


def plant(array, rng, least, largest):
    longest = array.shape.index(max(array.shape))
    spots = []
    for shift in (0, 1):
        where = [jax.random.randint(jax.random.fold_in(rng, axis), (), 0, length) for axis, length in enumerate(array.shape)]
        where[longest] = (where[longest] + shift) % array.shape[longest]
        spots.append(tuple(where))
    return array.at[spots[0]].set(least).at[spots[1]].set(largest)


def raised(array, stream_key, source, target, parts, factor):
    owner, partner = [(jnp.arange(array.shape[dim]) // (array.shape[dim] // parts)).reshape([-1 if axis == dim else 1 for axis in range(array.ndim)]) for dim in (source, target)]
    chosen = jax.random.permutation(stream_key, parts)[partner]
    strong = (owner == chosen) | (owner == (partner + parts // 2) % parts)
    return jnp.where(strong, factor * array, array)


def shard_levels(key, extent, split, least, largest):
    gain = 1.0
    for axis_at, shards_of in split:
        steps = jax.random.uniform(jax.random.fold_in(jax.random.fold_in(key, 6), axis_at), (shards_of,), jnp.float32, least / len(split), largest / len(split))
        gain = gain * jnp.repeat(jnp.exp(steps), extent[axis_at] // shards_of).reshape((-1,) + (1,) * (len(extent) - 1 - axis_at))
    return gain


def deal_out(rng, own, number, rows, number_of, top, reach, skew):
    sequence = jax.random.permutation(rng, number_of)
    heavy_load, usual = portions_of(number_of, rows * top, reach, skew, True), portions_of(number_of, rows * top, reach, skew, False)
    places = jnp.arange(number_of)

    def named(tallies, offset_by):
        used = int((tallies > 0).sum())
        fixed = max(1, used // 4)
        moved = fixed + (places - fixed + offset_by * (used - fixed)) % max(1, number_of - fixed)
        return jnp.zeros((number_of,), jnp.int32).at[sequence[jnp.where(places < fixed, places, moved)]].set(jnp.asarray(tallies, jnp.int32))

    tallies = jnp.where(number % 4 == 0, named(heavy_load, number // 4), named(usual, number - number // 4 - 1))
    mixed = jax.random.permutation(jax.random.fold_in(own, 3), number_of)
    source_of, receiver = mixed[0:number_of // 2 * 2:2], mixed[1:number_of // 2 * 2:2]
    margin = jnp.minimum(tallies[source_of] - 1, reach - tallies[receiver]) // 2
    margin = jnp.where((source_of == sequence[0]) | (receiver == sequence[0]) | (tallies[receiver] == 0), 0, jnp.maximum(margin, 0))
    moved = jax.random.randint(jax.random.fold_in(own, 4), (number_of // 2,), 0, 1 << 20) % (margin + 1)
    tallies = tallies.at[source_of].add(-moved).at[receiver].add(moved)
    members = jnp.searchsorted(jnp.cumsum(tallies), jnp.arange(rows * top), side="right").astype(jnp.int32)
    listing = members.reshape(top, rows).T
    listing = listing[jax.random.permutation(jax.random.fold_in(own, 1), rows)]
    offset_by = jax.random.randint(jax.random.fold_in(own, 2), (rows, 1), 0, top)
    return jnp.take_along_axis(listing, (jnp.arange(top)[None, :] + offset_by) % top, axis=1)


def portions_of(amount, total, limit, lean, full):
    weights = [(1 << 20) // math.isqrt(grade ** lean) + 1 for grade in range(1, amount + 1)]
    largest = limit if full else min(limit, max(-(-total // amount), total * weights[0] // sum(weights)))
    least = 1 if total - largest >= amount - 1 else 0
    given, surplus = [largest] + [least] * (amount - 1), total - largest - least * (amount - 1)
    while surplus > 0:
        movable = [i for i in range(1, amount) if given[i] < largest] or [i for i in range(1, amount) if given[i] < limit]
        pool, budget = sum([weights[i] for i in movable]), surplus
        for i in movable:
            extra = min(limit - given[i], max(1, budget * weights[i] // pool), surplus)
            given[i] = given[i] + extra
            surplus = surplus - extra
    return np.array(given)


def centred(stream_key, extent, width, most, split=(), kind=jnp.bfloat16):
    values = width * jax.random.normal(stream_key, extent, jnp.float32)
    if split:
        values = values * shard_levels(stream_key, extent, split, -0.22, 0.18)
    return jnp.clip(values, -most, most).astype(kind)


def noise_with(key, extent, scale, most, cuts, heavy, kind=jnp.bfloat16):
    result = scale * jax.random.normal(key, extent, jnp.float32)
    if cuts:
        result = result * shard_levels(key, extent, cuts, -0.22, 0.18)
    return jnp.clip(raised(result, jax.random.fold_in(key, 3), *heavy), -most, most).astype(kind)


def setup_inputs(seed: int = 0) -> dict:
    seeds = jax.random.split(jax.random.key(seed), 10)
    tokens = noise_with(seeds[0], (TOKENS, D), 1.0, 24.0, ((0, 128),), (0, 1, 128, 5.5))
    cotangent = centred(seeds[1], (TOKENS, D), 1.0, 6.0, ((0, 128),))
    router = centred(seeds[2], (D, EXPERTS), D ** -0.5, 0.09375)
    picks_keys = jax.random.split(jax.random.fold_in(seeds[3], 1), TOKENS // TOK_DEV)
    picks_turns = jax.random.permutation(jax.random.fold_in(seeds[3], 3), TOKENS // TOK_DEV)
    picks = jax.vmap(lambda own, number: deal_out(jax.random.fold_in(seeds[3], 2), own, number, TOK_DEV, EXPERTS, TOP, CAP, 1))(picks_keys, picks_turns).reshape((TOKENS, TOP))
    language = plant(jax.random.randint(seeds[4], (TOKENS,), 0, LANGS), jax.random.fold_in(seeds[4], 1), 0, LANGS - 1).astype(jnp.int32)
    teacher = jnp.clip(jax.random.uniform(seeds[5], (LANGS, EXPERTS), jnp.float32, 0.02, 0.98), 0.02, 0.98)
    w_gate = centred(seeds[6], (EXPERTS, D, FF), D ** -0.5, 0.09375, ((0, 128),))
    w_up = centred(seeds[7], (EXPERTS, D, FF), D ** -0.5, 0.09375, ((0, 128),))
    w_down = centred(seeds[8], (EXPERTS, FF, D), FF ** -0.5, 0.1875, ((0, 128),))
    return {"tokens": tokens, "cotangent": cotangent, "router": router, "picks": picks, "language": language, "teacher": teacher, "w_gate": w_gate, "w_up": w_up, "w_down": w_down}


ROUTE_SCALE = 2.5

def silu_parts(values):
    sigma = jax.nn.sigmoid(values)
    return (values * sigma, sigma * (1.0 + values * (1.0 - sigma)))

def slots_of(block_picks):
    flat = block_picks.reshape(-1)
    one_hot = (flat[:, None] == jnp.arange(EXPERTS, dtype=jnp.int32)[None, :]).astype(jnp.int32)
    before = jnp.cumsum(one_hot, axis=0) - one_hot
    return lax.optimization_barrier(jnp.sum(before * one_hot, axis=1)).astype(jnp.int32)

def expert_backward(rows_in, rows_cot, gate_w, up_w, down_w):
    gate_pre = jnp.dot(rows_in, gate_w, preferred_element_type=jnp.float32)
    up_pre = jnp.dot(rows_in, up_w, preferred_element_type=jnp.float32)
    back = jnp.dot(rows_cot, down_w.T, preferred_element_type=jnp.float32)
    active, slope = silu_parts(gate_pre)
    pick_grad = lax.optimization_barrier(jnp.sum(back * active * up_pre, axis=1)).astype(jnp.bfloat16)
    gate_grad = (back * up_pre * slope).astype(jnp.bfloat16)
    up_grad = (back * active).astype(jnp.bfloat16)
    expert_grad = (jnp.dot(gate_grad, gate_w.T, preferred_element_type=jnp.float32) + jnp.dot(up_grad, up_w.T, preferred_element_type=jnp.float32)).astype(jnp.bfloat16)
    return (expert_grad, pick_grad)

def reference(tokens, cotangent, router, picks, language, teacher, w_gate, w_up, w_down):
    logits = jnp.dot(tokens, router, preferred_element_type=jnp.float32)
    scores = jax.nn.sigmoid(logits)
    picked = jnp.take_along_axis(scores, picks, axis=1)
    route_w = ROUTE_SCALE * picked / lax.optimization_barrier(jnp.sum(picked, axis=1, keepdims=True))
    lang_hot = (language[:, None] == jnp.arange(LANGS, dtype=jnp.int32)[None, :]).astype(jnp.float32)
    target = jnp.dot(lang_hot, teacher, precision=lax.Precision.HIGHEST)
    blocks = picks.reshape(DEVICES, TOK_DEV, TOP)
    slot_index = jax.vmap(slots_of)(blocks)
    position = blocks.reshape(DEVICES, TOK_DEV * TOP) * CAP + slot_index
    count_rows = TOK_DEV * TOP

    def place(pos_row):
        return jnp.full((EXPERTS * CAP,), -1, jnp.int32).at[pos_row].set(jnp.arange(count_rows, dtype=jnp.int32))
    slot_owner = jax.vmap(place)(position).reshape(DEVICES, EXPERTS, CAP).transpose(1, 0, 2)
    route_flat = route_w.reshape(DEVICES, count_rows)
    device_ids = jnp.broadcast_to(jnp.arange(DEVICES, dtype=jnp.int32)[:, None], (DEVICES, CAP))

    def per_expert(carry, inputs):
        token_acc, pick_all = carry
        owner_rows, gate_w, up_w, down_w = inputs
        is_valid = owner_rows >= 0
        safe_owner = jnp.maximum(owner_rows, 0).astype(jnp.int32)
        token_ids = (device_ids * TOK_DEV + safe_owner // TOP).reshape(-1).astype(jnp.int32)
        valid_flat = is_valid.reshape(-1)
        rows_in = jnp.where(valid_flat[:, None], tokens[token_ids], jnp.zeros((), tokens.dtype))
        rows_cot = jnp.where(valid_flat[:, None], cotangent[token_ids], jnp.zeros((), cotangent.dtype))
        expert_grad, pick_grad = expert_backward(rows_in, rows_cot, gate_w, up_w, down_w)
        weight_rows = jnp.where(is_valid, route_flat[device_ids, safe_owner], jnp.zeros((), jnp.float32)).reshape(-1)
        token_acc = token_acc.at[token_ids].add(weight_rows[:, None] * expert_grad.astype(jnp.float32))
        target_rows = jnp.where(is_valid, safe_owner, count_rows).astype(jnp.int32)
        pick_all = pick_all.at[device_ids, target_rows].set(pick_grad.astype(jnp.float32).reshape(DEVICES, CAP), mode='drop')
        return ((token_acc, pick_all), None)
    start = (jnp.zeros((TOKENS, D), jnp.float32), jnp.zeros((DEVICES, count_rows), jnp.float32))
    (token_acc, pick_all), _ = lax.scan(per_expert, start, (slot_owner, w_gate, w_up, w_down))
    back_pick = pick_all.reshape(TOKENS, TOP)
    mixed = lax.optimization_barrier(jnp.sum(route_w * back_pick, axis=1, keepdims=True))
    per_pick = route_w * (1.0 - picked) * (back_pick - mixed / ROUTE_SCALE)
    pick_hot = (picks[:, :, None] == jnp.arange(EXPERTS, dtype=jnp.int32)[None, None, :]).astype(jnp.float32)
    gate_dlogit = jnp.einsum('tk,tke->te', per_pick, pick_hot).astype(jnp.bfloat16)
    kd_dlogit = (scores - target).astype(jnp.bfloat16)
    router_part = jnp.dot(kd_dlogit, router.T, preferred_element_type=jnp.float32) + jnp.dot(gate_dlogit, router.T, preferred_element_type=jnp.float32)
    token_grad = (token_acc + router_part).astype(jnp.bfloat16)
    router_grad = (jnp.dot(tokens.T, kd_dlogit, preferred_element_type=jnp.float32) + jnp.dot(tokens.T, gate_dlogit, preferred_element_type=jnp.float32)) / math.sqrt(TOKENS)
    return (token_grad, router_grad)
```

```python
import math

import jax
import jax.numpy as jnp
import numpy as np
from jax import lax
from jax.experimental import pallas as pl
from jax.experimental.pallas import tpu as pltpu
from jax.sharding import PartitionSpec as P

D, FF, E, T, LANGS, TOP = 3584, 1024, 128, 32, 8, 8
ROUTE_SCALE = 2.5
MESH = pl.DeviceIdType.MESH
BF, F32 = jnp.bfloat16, jnp.float32
CHUNKS = ((0, 640), (1, 640), (2, 512))
BASE = tuple(sum(2 * c for _, c in CHUNKS[:i]) for i in range(len(CHUNKS)))
NC = len(CHUNKS)
ROWS = 384
NT = (((1,), (1,)), ((), ()))
TN = (((0,), (0,)), ((), ()))


def xyz_of(axis, u, v, w):
    return ((v, w, u), (v, u, w), (u, v, w))[axis]


def uvw_of(axis, x, y, z):
    return ((z, x, y), (y, x, z), (x, y, z))[axis]


def tables():
    perm = np.zeros((2, ROWS, ROWS), np.float32)
    for x in range(4):
        for y in range(4):
            for z in range(4):
                for s in range(6):
                    row = (x * 4 + y) * 24 + z * 6 + s
                    for axis in (1, 2):
                        u, v, w = uvw_of(axis, x, y, z)
                        perm[axis - 1, row, (v * 4 + w) * 24 + u * 6 + s] = 1
    select = np.zeros((2 * E, 12 * 128), np.float32)
    for axis in range(3):
        for u in range(4):
            for v in range(4):
                for w in range(4):
                    for k in range(2):
                        x, y, z = xyz_of(axis, u, v, w)
                        expert, j = 32 * z + 8 * x + 2 * y + k, v * 8 + w * 2 + k
                        at = (axis * 4 + u) * 128
                        select[expert, at + j] = 1
                        select[E + expert, at + 32 + j] = 1
    row, lane = np.arange(768)[:, None], np.arange(128)[None, :]
    spread = np.stack([row // 24 == lane, row // 24 + 32 == lane]).astype(np.float32)
    own, col = row % 24 // 3, np.arange(256)[None, :] // 32
    slot = np.where(own == col, row % 3 + 1, 9).astype(np.float32)
    short = np.arange(ROWS)[:, None]
    half = np.stack([short // 24 * 2 + k == lane for k in range(2)]).astype(np.float32)
    as_bf = lambda array: jnp.asarray(array, BF)
    return (as_bf(perm), as_bf(perm.transpose(0, 2, 1)), as_bf(select), as_bf(spread), as_bf(slot), as_bf(slot.T), as_bf(half))


def dot(a, b):
    return jnp.dot(a, b, preferred_element_type=F32)


def dot_nt(a, b):
    return lax.dot_general(a, b, NT, preferred_element_type=F32)


def dot_tn(a, b):
    return lax.dot_general(a, b, TN, preferred_element_type=F32)


def ident(x, y, z, k):
    return (z * 2 + x // 2, (x % 2) * 8 + y * 2 + k)


def kernel(
    tokens, cotangent, router, picks, language, teacher, w_gate, w_up, w_down,
    perm, perm_t, select, spread, slot, slot_t, half,
    token_grad, router_grad,
    wg, wu, wd, rows, meta_out, meta_in, pick_l, mix_w, r1, out2, x2, xt, xc, grads,
    yin, part, back, pg_out, pg_in, bp_out, bp_in, route, extra, rgs, rgb, rk, s1, rz, s2, rx, s3, ry,
    w_sem, in_sem, r1_s, r1_r, meta_s, meta_r, x2_s, x2_r, y_s, y_r, part_s, part_r, pg_s, pg_r, bp_s, bp_r, rg_s, rg_r,
):
    me_row, me_col = lax.axis_index("row"), lax.axis_index("col")
    x, y, z, k = (me_row % 2) * 2 + me_col // 8, (me_col // 2) % 4, me_row // 2, me_col % 2
    places = [uvw_of(axis, x, y, z) for axis in range(3)]

    def device(axis, u, v, w, core):
        return ident(*xyz_of(axis, u, v, w), core)

    def remote(src, dst, send, recv, where):
        return pltpu.make_async_remote_copy(
            src_ref=src, dst_ref=dst, send_sem=send, recv_sem=recv, device_id=where, device_id_type=MESH
        )

    def arrived(ref, sem):
        pltpu.make_async_copy(ref, ref, sem).wait()

    weights = [
        pltpu.make_async_copy(src.at[0], dst, w_sem.at[i])
        for i, (src, dst) in enumerate(((w_gate, wg), (w_up, wu), (w_down, wd)))
    ]
    inputs = [
        pltpu.make_async_copy(src, rows.at[i], in_sem.at[i]) for i, src in enumerate((tokens, cotangent))
    ]
    for copy in inputs + weights:
        copy.start()
    barrier = pltpu.get_barrier_semaphore()

    def greet(dx, dy, dz, dk):
        where = ident((x + dx) % 4, (y + dy) % 4, (z + dz) % 4, (k + dk) % 2)
        pl.semaphore_signal(barrier, inc=1, device_id=where, device_id_type=MESH)

    def greet_z(i, _):
        greet(i // 8, (i // 2) % 4, 0, i % 2)
        return 0

    def greet_y(i, _):
        greet(i // 6, 0, 1 + (i // 2) % 3, i % 2)
        return 0

    def greet_x(i, _):
        greet(0, 1 + i // 6, 1 + (i // 2) % 3, i % 2)
        return 0

    lax.fori_loop(1, 32, greet_z, 0)
    lax.fori_loop(0, 24, greet_y, 0)
    lax.fori_loop(0, 18, greet_x, 0)

    experts = lax.broadcasted_iota(jnp.int32, (T, E), 1)
    picked = jnp.zeros((T, E), F32)
    for i in range(TOP):
        picked += jnp.where(picks[:, i : i + 1] == experts, 1.0, 0.0)
    before = lax.broadcasted_iota(jnp.int32, (T, T), 1) < lax.broadcasted_iota(jnp.int32, (T, T), 0)
    rank = dot(jnp.where(before, 1.0, 0.0).astype(BF), picked.astype(BF))
    code = picked * (rank + 1.0)

    for copy in inputs:
        copy.wait()
    pl.semaphore_wait(barrier, 73)

    for i, (axis, wide) in enumerate(CHUNKS):
        u, v, w = places[axis]
        mine = u * 2 + k

        def hop(s, _, i=i, axis=axis, wide=wide, u=u, v=v, w=w, mine=mine):
            du, core = s // 2, (k + s) % 2
            start = pl.multiple_of(BASE[i] + core * wide, 128)
            remote(
                rows.at[:, :, pl.ds(start, wide)], r1[i].at[:, mine], r1_s.at[i], r1_r.at[i],
                device(axis, (u + du) % 4, v, w, core),
            ).start()
            return 0

        lax.fori_loop(1, 8, hop, 0)
        start = pl.multiple_of(BASE[i] + k * wide, 128)
        pltpu.make_async_copy(rows.at[:, :, pl.ds(start, wide)], r1[i].at[:, mine], r1_r.at[i]).start()

    logits = dot(rows[0], router[...])
    scores = jax.nn.sigmoid(logits)
    chosen = picked * scores
    weight = ROUTE_SCALE * chosen / jnp.sum(chosen, axis=1, keepdims=True)
    route[0] = weight
    route[1] = weight * (1.0 - scores)
    told = dot(code.astype(BF), select[0:E, :]) + dot(weight.astype(BF), select[E:, :])
    for m in range(12):
        meta_out[m] = told[:, m * 128 : (m + 1) * 128].astype(BF)
    for axis in range(3):
        u, v, w = places[axis]
        mine = u * 2 + k

        def tell(s, _, axis=axis, u=u, v=v, w=w, mine=mine):
            to = (u + s // 2) % 4
            core = (k + s) % 2
            remote(
                meta_out.at[axis * 4 + to], meta_in.at[axis, mine], meta_s.at[axis], meta_r.at[axis],
                device(axis, to, v, w, core),
            ).start()
            return 0

        lax.fori_loop(1, 8, tell, 0)
        pltpu.make_async_copy(meta_out.at[axis * 4 + u], meta_in.at[axis, mine], meta_r.at[axis]).start()

    target = jnp.zeros((T, E), F32)
    for i in range(LANGS):
        target += jnp.where(language[...] == i, teacher[i : i + 1, :], 0.0)
    route[2] = scores - target

    for i, (axis, wide) in enumerate(CHUNKS):
        arrived(meta_in.at[axis], meta_r.at[axis])
        codes = meta_in[axis].reshape(256, 128)
        pick_l[axis] = jnp.where(dot_nt(spread[0], codes) == slot[...].astype(F32), 1.0, 0.0).astype(BF)
        arrived(r1[i], r1_r.at[i])

        def gather(g, _, i=i, axis=axis, wide=wide):
            lhs = pick_l[axis, pl.ds(pl.multiple_of(g * 192, 192), 192), :]
            for a in range(2):
                got = dot(lhs, r1[i][a].reshape(256, wide)).astype(BF)
                out2[i][pl.ds(g * 8, 8), a * 24 : a * 24 + 24, :] = got.reshape(8, 24, wide)
            return 0

        lax.fori_loop(0, 4, gather, 0)

    def offsets(s):
        j = s % 16
        return j % 4, (j // 4 + j) % 4, s // 16

    def spread_out(s, _):
        dv, dw, dk = offsets(s)
        for i, (axis, wide) in enumerate(CHUNKS):
            u, v, w = places[axis]
            tv, tw, core = (v + dv) % 4, (w + dw) % 4, (k + dk) % 2
            remote(
                out2[i].at[tv * 8 + tw * 2 + core], x2[i].at[k, v * 4 + w], x2_s.at[i], x2_r.at[i],
                device(axis, u, tv, tw, core),
            ).start()
        return 0

    lax.fori_loop(1, 32, spread_out, 0)
    for i, (axis, wide) in enumerate(CHUNKS):
        u, v, w = places[axis]
        pltpu.make_async_copy(out2[i].at[v * 8 + w * 2 + k], x2[i].at[k, v * 4 + w], x2_r.at[i]).start()

    for axis in range(3):
        codes = meta_in[axis].reshape(256, 128)
        mix_w[axis] = jnp.where(
            dot_nt(codes, spread[0]) == slot_t[...].astype(F32), dot_nt(codes, spread[1]), 0.0
        ).astype(BF)

    for i, (axis, wide) in enumerate(CHUNKS):
        arrived(x2[i], x2_r.at[i])
        for q in range(2):
            cols = slice(BASE[i] + q * wide, BASE[i] + (q + 1) * wide)
            for a in range(2):
                got = x2[i][q, :, a * 24 : a * 24 + 24, :].reshape(ROWS, wide)
                got = got if axis == 0 else dot(perm[axis - 1], got).astype(BF)
                if a == 0:
                    xt[:, cols] = got
                else:
                    xc[:, :, cols] = got.reshape(16, 24, wide)
    for copy in weights:
        copy.wait()

    def hidden(n, total):
        cols = pl.ds(pl.multiple_of(n * 256, 256), 256)
        gate = dot(xt[...], wg[:, cols])
        up = dot(xt[...], wu[:, cols])
        into = dot_nt(xc[...].reshape(ROWS, D), wd[cols, :])
        sigma = jax.nn.sigmoid(gate)
        active = gate * sigma
        up_part = into * active
        grads[:, cols] = (into * up * (sigma * (1.0 + gate * (1.0 - sigma)))).astype(BF)
        grads[:, pl.ds(pl.multiple_of(FF + n * 256, 256), 256)] = up_part.astype(BF)
        return total + jnp.sum(up_part * up, axis=1, keepdims=True)

    pick_grad = lax.fori_loop(0, FF // 256, hidden, jnp.zeros((ROWS, 1), F32))
    pg_out[...] = jnp.broadcast_to(pick_grad, (ROWS, 128)).astype(BF).reshape(16, 24, 128)

    def send_pick(s, _):
        dv, dw, _ = offsets(s)
        tx, ty = (x + dv) % 4, (y + dw) % 4
        remote(pg_out.at[tx * 4 + ty], pg_in.at[x * 4 + y], pg_s, pg_r, ident(tx, ty, z, k)).start()
        return 0

    lax.fori_loop(1, 16, send_pick, 0)
    pltpu.make_async_copy(pg_out.at[x * 4 + y], pg_in.at[x * 4 + y], pg_r).start()

    for i, (axis, wide) in enumerate(CHUNKS):
        u, v, w = places[axis]
        if axis == 0:
            lhs = grads
        else:
            lhs = xt.at[:, 0 : 2 * FF]
            lhs[...] = dot(perm_t[axis - 1], grads[...]).astype(BF)
        for dq in range(2):
            q = (k + dq) % 2
            cols = pl.ds(pl.multiple_of(BASE[i] + q * wide, 128), wide)
            got = dot_nt(lhs[:, :FF], wg[cols, :]) + dot_nt(lhs[:, FF:], wu[cols, :])
            xc[:, :, cols] = got.astype(BF).reshape(16, 24, wide)

            def give(s, _, i=i, axis=axis, u=u, v=v, w=w, q=q, cols=cols):
                dv, dw, _ = offsets(s)
                tv, tw = (v + dv) % 4, (w + dw) % 4
                remote(
                    xc.at[tv * 4 + tw, :, cols], yin[i].at[v * 8 + w * 2 + k], y_s.at[i], y_r.at[i],
                    device(axis, u, tv, tw, q),
                ).start()
                return 0

            lax.fori_loop(1 - dq, 16, give, 0)
            if dq == 0:
                pltpu.make_async_copy(xc.at[v * 4 + w, :, cols], yin[i].at[v * 8 + w * 2 + k], y_r.at[i]).start()

    arrived(pg_in, pg_r)
    codes = meta_in[0].reshape(256, 128)
    wanted = jnp.where(dot_nt(codes, half[k]) == slot_t[:, :ROWS].astype(F32), 1.0, 0.0).astype(BF)
    line = lax.broadcasted_iota(jnp.int32, (ROWS, 128), 0)
    owner = 32 * z + 2 * ((line * 2731) >> 16) + k
    values = jnp.where(
        lax.broadcasted_iota(jnp.int32, (ROWS, 128), 1) == owner, pg_in[...].reshape(ROWS, 128).astype(F32), 0.0
    ).astype(BF)
    bp_out[...] = dot(wanted, values).astype(BF).reshape(8, T, 128)

    def send_dense(s, _):
        to, core = (z + s // 2) % 4, (k + s) % 2
        remote(bp_out.at[to * 2 + core], bp_in.at[z * 2 + k], bp_s, bp_r, ident(x, y, to, core)).start()
        return 0

    lax.fori_loop(1, 8, send_dense, 0)
    pltpu.make_async_copy(bp_out.at[z * 2 + k], bp_in.at[z * 2 + k], bp_r).start()

    arrived(bp_in, bp_r)
    pick_back = jnp.sum(bp_in[...].astype(F32), axis=0)
    mixed = jnp.sum(route[0] * pick_back, axis=1, keepdims=True)
    gate_dlogit = (route[1] * (pick_back - mixed / ROUTE_SCALE)).astype(BF)
    kd_dlogit = route[2].astype(BF)
    extra[...] = dot_nt(kd_dlogit, router[...]) + dot_nt(gate_dlogit, router[...])

    rgs[896:, :] = jnp.zeros((8, 128), F32)
    for zq in range(4):
        mine = rows[0, :, zq * 896 : (zq + 1) * 896]
        rgs[0:896, :] = dot_tn(mine, kd_dlogit) + dot_tn(mine, gate_dlogit)
        for g in range(32):
            rgb[g % 2, zq * 16 + g // 2] = rgs[28 * g : 28 * g + 32, :].astype(BF)
    to_core = remote(rgb.at[1 - k], rk, rg_s.at[0], rg_r.at[0], ident(x, y, z, 1 - k))
    to_core.start()

    def combine(i):
        axis, wide = CHUNKS[i]
        u, v, w = places[axis]
        arrived(yin[i], y_r.at[i])
        part[i][...] = dot(mix_w[axis], yin[i][...].reshape(768, wide)).astype(BF).reshape(8, T, wide)

        def give_back(s, _):
            to, core = (u + s // 2) % 4, (k + s) % 2
            remote(
                part[i].at[to * 2 + core], back[i].at[k, u], part_s.at[i], part_r.at[i], device(axis, to, v, w, core)
            ).start()
            return 0

        lax.fori_loop(1, 8, give_back, 0)
        pltpu.make_async_copy(part[i].at[u * 2 + k], back[i].at[k, u], part_r.at[i]).start()

    to_core.wait_recv()
    s1[...] = (rgb[k].astype(F32) + rk[...].astype(F32)).astype(BF)

    def scatter(source, count, into, at, step, where):
        def one(d, _):
            to = (at + d) % 4
            remote(
                source.at[pl.ds(to * count, count)], into.at[at], rg_s.at[step], rg_r.at[step], where(to)
            ).start()
            return 0

        lax.fori_loop(1, 4, one, 0)
        pltpu.make_async_copy(source.at[pl.ds(at * count, count)], into.at[at], rg_r.at[step]).start()

    scatter(s1, 16, rz, z, 1, lambda to: ident(x, y, to, k))
    combine(0)
    arrived(rz, rg_r.at[1])
    s2[...] = jnp.sum(rz[...].astype(F32), axis=0)
    scatter(s2, 4, rx, x, 2, lambda to: ident(to, y, z, k))
    combine(1)
    arrived(rx, rg_r.at[2])
    s3[...] = jnp.sum(rx[...], axis=0)
    scatter(s3, 1, ry, y, 3, lambda to: ident(x, to, z, k))
    combine(2)
    arrived(ry, rg_r.at[3])
    router_grad[...] = jnp.sum(ry[...], axis=(0, 1))[:28, :] / math.sqrt(E * T)

    for i, (axis, wide) in enumerate(CHUNKS):
        arrived(back[i], part_r.at[i])
        for q in range(2):
            cols = slice(BASE[i] + q * wide, BASE[i] + (q + 1) * wide)
            token_grad[:, cols] = (jnp.sum(back[i][q].astype(F32), axis=0) + extra[:, cols]).astype(BF)

    for i in range(NC):
        arrived(r1[i].at[:, pl.ds(0, 7)], r1_s.at[i])
        arrived(x2[i].at[0], x2_s.at[i])
        arrived(x2[i].at[0, pl.ds(0, 15)], x2_s.at[i])
        arrived(yin[i].at[pl.ds(0, 31)], y_s.at[i])
        arrived(part[i].at[pl.ds(0, 7)], part_s.at[i])
    for axis in range(3):
        arrived(meta_in.at[axis, pl.ds(0, 7)], meta_s.at[axis])
    arrived(pg_in.at[pl.ds(0, 15)], pg_s)
    arrived(bp_in.at[pl.ds(0, 7)], bp_s)
    to_core.wait_send()
    arrived(rz.at[pl.ds(0, 3)], rg_s.at[1])
    arrived(rx.at[pl.ds(0, 3)], rg_s.at[2])
    arrived(ry.at[pl.ds(0, 3)], rg_s.at[3])


def local(tokens, cotangent, router, picks, language, teacher, w_gate, w_up, w_down):
    vmem, anywhere = pl.BlockSpec(memory_space=pltpu.VMEM), pl.BlockSpec(memory_space=pl.ANY)
    buf, sem = pltpu.VMEM, pltpu.SemaphoreType.DMA
    per = lambda make: tuple(buf(make(wide), BF) for _, wide in CHUNKS)
    scratch = [
        buf((D, FF), BF), buf((D, FF), BF), buf((FF, D), BF),
        buf((2, T, D), BF),
        buf((12, T, 128), BF), buf((3, 8, T, 128), BF),
        buf((3, 768, 256), BF), buf((3, 256, 768), BF),
        per(lambda c: (2, 8, T, c)),
        per(lambda c: (32, 48, c)), per(lambda c: (2, 16, 48, c)),
        buf((ROWS, D), BF), buf((16, 24, D), BF),
        buf((ROWS, 2 * FF), BF),
        per(lambda c: (32, 24, c)),
        per(lambda c: (8, T, c)), per(lambda c: (2, 4, T, c)),
        buf((16, 24, 128), BF), buf((16, 24, 128), BF),
        buf((8, T, 128), BF), buf((8, T, 128), BF),
        buf((3, T, E), F32), buf((T, D), F32),
        buf((904, 128), F32), buf((2, 64, 32, 128), BF), buf((64, 32, 128), BF),
        buf((64, 32, 128), BF), buf((4, 16, 32, 128), BF),
        buf((16, 32, 128), F32), buf((4, 4, 32, 128), F32),
        buf((4, 32, 128), F32), buf((4, 1, 32, 128), F32),
        sem((3,)), sem((2,)),
        sem((NC,)), sem((NC,)), sem((3,)), sem((3,)), sem((NC,)), sem((NC,)), sem((NC,)), sem((NC,)), sem((NC,)), sem((NC,)),
        sem, sem, sem, sem, sem((4,)), sem((4,)),
    ]
    return pl.pallas_call(
        kernel,
        out_shape=(jax.ShapeDtypeStruct((T, D), BF), jax.ShapeDtypeStruct((28, 128), F32)),
        in_specs=[anywhere, anywhere, vmem, vmem, vmem, vmem, anywhere, anywhere, anywhere] + [vmem] * 7,
        out_specs=(vmem, vmem),
        scratch_shapes=scratch,
        compiler_params=pltpu.CompilerParams(
            collective_id=0, has_side_effects=True, vmem_limit_bytes=60 << 20
        ),
        cost_estimate=pl.CostEstimate(flops=15_000_000_000, bytes_accessed=24_000_000, transcendentals=400_000),
    )(tokens, cotangent, router, picks, language.reshape(T, 1), teacher, w_gate, w_up, w_down, *tables())


def solution(mesh):
    split = P(("row", "col"), None)
    cube = P(("row", "col"), None, None)
    return jax.shard_map(
        local,
        mesh=mesh,
        in_specs=(split, split, P(), split, P(("row", "col")), P(), cube, cube, cube),
        out_specs=(split, split),
        check_vma=False,
    )
```

```python
import math

import jax
import jax.numpy as jnp
import numpy as np
from jax import lax
from jax.experimental import pallas as pl
from jax.experimental.pallas import tpu as pltpu
from jax.sharding import PartitionSpec as P

D, FF, E, T, LANGS, TOP = 3584, 1024, 128, 32, 8, 8
ROUTE_SCALE = 2.5
MESH = pl.DeviceIdType.MESH
BF, F32 = jnp.bfloat16, jnp.float32
CHUNKS = ((0, 128), (1, 128), (2, 128), (0, 384), (1, 384), (2, 256), (0, 128), (1, 128), (2, 128))
SETS = ((0, 1, 2), (3, 4, 5), (6, 7, 8))
BASE = tuple(sum(2 * c for _, c in CHUNKS[:i]) for i in range(len(CHUNKS)))
NC = len(CHUNKS)
RETURN = ((0, 512), (1, 512), (2, 384), (0, 128), (1, 128), (2, 128))
RBASE = tuple(sum(2 * c for _, c in RETURN[:i]) for i in range(len(RETURN)))
NR = len(RETURN)
ROWS = 384
FIRST = BASE[SETS[2][0]]
NT = (((1,), (1,)), ((), ()))
TN = (((0,), (0,)), ((), ()))


def xyz_of(axis, u, v, w):
    return ((v, w, u), (v, u, w), (u, v, w))[axis]


def uvw_of(axis, x, y, z):
    return ((z, x, y), (y, x, z), (x, y, z))[axis]


def tables():
    perm = np.zeros((2, ROWS, ROWS), np.float32)
    for x in range(4):
        for y in range(4):
            for z in range(4):
                for s in range(6):
                    row = (x * 4 + y) * 24 + z * 6 + s
                    for axis in (1, 2):
                        u, v, w = uvw_of(axis, x, y, z)
                        perm[axis - 1, row, (v * 4 + w) * 24 + u * 6 + s] = 1
    select = np.zeros((2 * E, 12 * 128), np.float32)
    for axis in range(3):
        for u in range(4):
            for v in range(4):
                for w in range(4):
                    for k in range(2):
                        x, y, z = xyz_of(axis, u, v, w)
                        expert, j = 32 * z + 8 * x + 2 * y + k, v * 8 + w * 2 + k
                        at = (axis * 4 + u) * 128
                        select[expert, at + j] = 1
                        select[E + expert, at + 32 + j] = 1
    row, lane = np.arange(768)[:, None], np.arange(128)[None, :]
    eye = np.eye(E, dtype=np.float32)
    spread = np.stack([row // 24 == lane, row // 24 + 32 == lane]).astype(np.float32)
    own, col = row % 24 // 3, np.arange(256)[None, :] // 32
    slot = np.where(own == col, row % 3 + 1, 9).astype(np.float32)
    short = np.arange(ROWS)[:, None]
    half = np.stack([short // 24 * 2 + k == lane for k in range(2)]).astype(np.float32)
    as_bf = lambda array: jnp.asarray(array, BF)
    return (as_bf(perm), as_bf(select), as_bf(spread), as_bf(slot[:24]), as_bf(slot[:ROWS].T), as_bf(half), as_bf(eye))


def dot(a, b):
    return jnp.dot(a, b, preferred_element_type=F32)


def dot_nt(a, b):
    return lax.dot_general(a, b, NT, preferred_element_type=F32)


def dot_tn(a, b):
    return lax.dot_general(a, b, TN, preferred_element_type=F32)


def ident(x, y, z, k):
    return (z * 2 + x // 2, (x % 2) * 8 + y * 2 + k)


def kernel(
    tokens, cotangent, router, picks, language, teacher, w_gate, w_up, w_down,
    perm, select_hbm, spread, slot, slot_t, half, eye,
    token_grad, router_grad,
    wg, wu, wd, rows, meta_out, meta_in, pick_l, mix_w, r1, out2, x2, xt, xc, acc, grads,
    yin, part, back, pg_out, pg_in, bp_out, bp_in, route, extra, rgs, rgb, rk, s1, rz, s2, rx,
    ready, w_sem, in_sem, r1_s, r1_r, meta_s, meta_r, x2_s, x2_r, y_s, y_r, part_s, part_r, pg_s, pg_r, bp_s, bp_r, rg_s, rg_r,
):
    me_row, me_col = lax.axis_index("row"), lax.axis_index("col")
    x, y, z, k = (me_row % 2) * 2 + me_col // 8, (me_col // 2) % 4, me_row // 2, me_col % 2
    places = [uvw_of(axis, x, y, z) for axis in range(3)]

    def device(axis, u, v, w, core):
        return ident(*xyz_of(axis, u, v, w), core)

    def remote(src, dst, send, recv, where):
        return pltpu.make_async_remote_copy(
            src_ref=src, dst_ref=dst, send_sem=send, recv_sem=recv, device_id=where, device_id_type=MESH
        )

    def arrived(ref, sem):
        pltpu.make_async_copy(ref, ref, sem).wait()

    weights = [
        pltpu.make_async_copy(src.at[0], dst, w_sem.at[i])
        for i, (src, dst) in enumerate(((w_gate, wg), (w_up, wu), (w_down, wd)))
    ]
    select = xt.at[0 : 2 * E, 0 : 12 * 128]
    inputs = [
        pltpu.make_async_copy(src, dst, in_sem.at[i])
        for i, (src, dst) in enumerate(((tokens, rows.at[0]), (cotangent, rows.at[1]), (select_hbm, select)))
    ]
    for copy in inputs + weights:
        copy.start()
    barrier = pltpu.get_barrier_semaphore()

    def greet(sem):
        for axis in range(3):
            u, v, w = places[axis]

            def one(s, _, axis=axis, u=u, v=v, w=w):
                where = device(axis, (u + s // 2) % 4, v, w, (k + s) % 2)
                pl.semaphore_signal(sem, inc=1, device_id=where, device_id_type=MESH)
                return 0

            lax.fori_loop(2 if axis else 1, 8, one, 0)

    greet(barrier)

    experts = lax.broadcasted_iota(jnp.int32, (E, T), 0)
    asked = jnp.zeros((E, T), F32)
    for i in range(TOP):
        asked += jnp.where(picks[i : i + 1, :] == experts, 1.0, 0.0)
    before = lax.broadcasted_iota(jnp.int32, (T, T), 0) < lax.broadcasted_iota(jnp.int32, (T, T), 1)
    rank = dot(asked.astype(BF), jnp.where(before, 1.0, 0.0).astype(BF))
    code = dot_tn((asked * (rank + 1.0)).astype(BF), eye[...])
    picked = jnp.where(code > 0.0, 1.0, 0.0)
    spoken = jnp.where(lax.broadcasted_iota(jnp.int32, (LANGS, T), 0) == language[...], 1.0, 0.0).astype(BF)
    target, left = jnp.zeros((T, E), F32), teacher[...]
    for _ in range(3):
        piece = left.astype(BF)
        left = left - piece.astype(F32)
        target += dot_tn(spoken, piece)

    for copy in inputs:
        copy.wait()
    logits = dot(rows[0], router[...])
    scores = jax.nn.sigmoid(logits)
    chosen = picked * scores
    weight = ROUTE_SCALE * chosen / jnp.sum(chosen, axis=1, keepdims=True)
    route[0] = weight
    route[1] = weight * (1.0 - scores)
    route[2] = scores - target
    told = dot(code.astype(BF), select[0:E, :]) + dot(weight.astype(BF), select[E:, :])
    for m in range(12):
        meta_out[m] = told[:, m * 128 : (m + 1) * 128].astype(BF)
    pl.semaphore_wait(barrier, 19)
    greet(ready)

    for axis in range(3):
        u, v, w = places[axis]
        mine = u * 2 + k

        def tell(s, _, axis=axis, u=u, v=v, w=w, mine=mine):
            to = (u + s // 2) % 4
            core = (k + s) % 2
            remote(
                meta_out.at[axis * 4 + to], meta_in.at[axis, mine], meta_s.at[axis], meta_r.at[axis],
                device(axis, to, v, w, core),
            ).start()
            return 0

        lax.fori_loop(1, 8, tell, 0)
        pltpu.make_async_copy(meta_out.at[axis * 4 + u], meta_in.at[axis, mine], meta_r.at[axis]).start()

    for i, (axis, wide) in enumerate(CHUNKS):
        u, v, w = places[axis]
        mine = u * 2 + k

        def hop(s, _, i=i, axis=axis, wide=wide, u=u, v=v, w=w, mine=mine):
            du, core = s // 2, (k + s) % 2
            start = pl.multiple_of(BASE[i] + core * wide, 128)
            remote(
                rows.at[:, :, pl.ds(start, wide)], r1[i].at[:, mine], r1_s.at[i], r1_r.at[i],
                device(axis, (u + du) % 4, v, w, core),
            ).start()
            return 0

        lax.fori_loop(1, 8, hop, 0)
        start = pl.multiple_of(BASE[i] + k * wide, 128)
        pltpu.make_async_copy(rows.at[:, :, pl.ds(start, wide)], r1[i].at[:, mine], r1_r.at[i]).start()

    def offsets(s):
        j = s % 16
        return j % 4, (j // 4 + j) % 4, s // 16

    for axis in range(3):
        arrived(meta_in.at[axis], meta_r.at[axis])
        codes = meta_in[axis].reshape(256, 128)
        slots = jnp.broadcast_to(slot[...].astype(F32)[None], (32, 24, 256)).reshape(768, 256)
        pick_l[axis] = jnp.where(dot_nt(spread[0], codes) == slots, 1.0, 0.0).astype(BF)

    def relay(chunks):
        for i in chunks:
            axis, wide = CHUNKS[i]
            arrived(r1[i], r1_r.at[i])

            def gather(g, _, i=i, axis=axis, wide=wide):
                lhs = pick_l[axis, pl.ds(pl.multiple_of(g * 192, 192), 192), :]
                for a in range(2):
                    got = dot(lhs, r1[i][a].reshape(256, wide)).astype(BF)
                    out2[i][pl.ds(g * 8, 8), a * 24 : a * 24 + 24, :] = got.reshape(8, 24, wide)
                return 0

            lax.fori_loop(0, 4, gather, 0)

        if chunks == SETS[0]:
            pl.semaphore_wait(ready, 19)

        def spread_out(s, _):
            dv, dw, dk = offsets(s)
            for i in chunks:
                axis, wide = CHUNKS[i]
                u, v, w = places[axis]
                tv, tw, core = (v + dv) % 4, (w + dw) % 4, (k + dk) % 2
                remote(
                    out2[i].at[tv * 8 + tw * 2 + core], x2[i].at[k, v * 4 + w], x2_s.at[i], x2_r.at[i],
                    device(axis, u, tv, tw, core),
                ).start()
            return 0

        lax.fori_loop(1, 32, spread_out, 0)
        for i in chunks:
            u, v, w = places[CHUNKS[i][0]]
            pltpu.make_async_copy(out2[i].at[v * 8 + w * 2 + k], x2[i].at[k, v * 4 + w], x2_r.at[i]).start()

    for chunks in SETS:
        relay(chunks)

    slots_t = jnp.concatenate([slot_t[...].astype(F32)] * 2, axis=1)
    for axis in range(3):
        codes = meta_in[axis].reshape(256, 128)
        mix_w[axis] = jnp.where(dot_nt(codes, spread[0]) == slots_t, dot_nt(codes, spread[1]), 0.0).astype(BF)

    def collect(chunks):
        for i in chunks:
            axis, wide = CHUNKS[i]
            arrived(x2[i], x2_r.at[i])
            for q in range(2):
                cols = slice(BASE[i] + q * wide, BASE[i] + (q + 1) * wide)
                for a in range(2):
                    got = x2[i][q, :, a * 24 : a * 24 + 24, :].reshape(ROWS, wide)
                    got = got if axis == 0 else dot(perm[axis - 1], got).astype(BF)
                    if a == 0:
                        xt[:, cols] = got
                    else:
                        xc[:, :, cols] = got.reshape(16, 24, wide)

    def parts(n, low, high):
        cols = pl.ds(pl.multiple_of(n * 256, 256), 256)
        gate = dot(xt[:, low:high], wg[low:high, cols])
        up = dot(xt[:, low:high], wu[low:high, cols])
        into = dot_nt(xc[:, :, low:high].reshape(ROWS, high - low), wd[cols, low:high])
        return cols, gate, up, into

    def first(n, _):
        cols, *values = parts(n, 0, FIRST)
        for i, value in enumerate(values):
            acc[i, :, cols] = value
        return 0

    def second(n, total):
        cols, gate, up, into = parts(n, FIRST, D)
        gate, up, into = acc[0, :, cols] + gate, acc[1, :, cols] + up, acc[2, :, cols] + into
        sigma = jax.nn.sigmoid(gate)
        active = gate * sigma
        up_part = into * active
        grads[:, cols] = (into * up * (sigma * (1.0 + gate * (1.0 - sigma)))).astype(BF)
        grads[:, pl.ds(pl.multiple_of(FF + n * 256, 256), 256)] = up_part.astype(BF)
        return total + jnp.sum(up_part * up, axis=1, keepdims=True)

    collect(SETS[0])
    collect(SETS[1])
    for copy in weights:
        copy.wait()
    lax.fori_loop(0, FF // 256, first, 0)
    collect(SETS[2])
    pick_grad = lax.fori_loop(0, FF // 256, second, jnp.zeros((ROWS, 1), F32))
    pg_out[...] = jnp.broadcast_to(pick_grad, (ROWS, 128)).astype(BF).reshape(16, 24, 128)

    def send_pick(s, _):
        dv, dw, _ = offsets(s)
        tx, ty = (x + dv) % 4, (y + dw) % 4
        remote(pg_out.at[tx * 4 + ty], pg_in.at[x * 4 + y], pg_s, pg_r, ident(tx, ty, z, k)).start()
        return 0

    lax.fori_loop(1, 16, send_pick, 0)
    pltpu.make_async_copy(pg_out.at[x * 4 + y], pg_in.at[x * 4 + y], pg_r).start()

    def permute(axis):
        if axis:
            xt[:, 0 : 2 * FF] = dot_tn(perm[axis - 1], grads[...]).astype(BF)

    def produce(i, dq):
        axis, wide = RETURN[i]
        cols = pl.ds(pl.multiple_of(RBASE[i] + (k + dq) % 2 * wide, 128), wide)
        lhs = xt if axis else grads
        got = dot_nt(lhs[:, :FF], wg[cols, :]) + dot_nt(lhs[:, FF : 2 * FF], wu[cols, :])
        xc[:, :, cols] = got.astype(BF).reshape(16, 24, wide)

    def give(i, dq):
        axis, wide = RETURN[i]
        u, v, w = places[axis]
        q = (k + dq) % 2
        cols = pl.ds(pl.multiple_of(RBASE[i] + q * wide, 128), wide)

        def one(s, _):
            dv, dw, _ = offsets(s)
            tv, tw = (v + dv) % 4, (w + dw) % 4
            remote(
                xc.at[tv * 4 + tw, :, cols], yin[i].at[v * 8 + w * 2 + k], y_s.at[i], y_r.at[i],
                device(axis, u, tv, tw, q),
            ).start()
            return 0

        lax.fori_loop(1 - dq, 16, one, 0)
        if dq == 0:
            pltpu.make_async_copy(xc.at[v * 4 + w, :, cols], yin[i].at[v * 8 + w * 2 + k], y_r.at[i]).start()

    def whole(i):
        for dq in range(2):
            produce(i, dq)
            give(i, dq)

    def combine(i):
        axis, wide = RETURN[i]
        u, v, w = places[axis]
        arrived(yin[i], y_r.at[i])
        part[i][...] = dot(mix_w[axis], yin[i][...].reshape(768, wide)).astype(BF).reshape(8, T, wide)

        def give_back(s, _):
            to, core = (u + s // 2) % 4, (k + s) % 2
            remote(
                part[i].at[to * 2 + core], back[i].at[k, u], part_s.at[i], part_r.at[i], device(axis, to, v, w, core)
            ).start()
            return 0

        lax.fori_loop(1, 8, give_back, 0)
        pltpu.make_async_copy(part[i].at[u * 2 + k], back[i].at[k, u], part_r.at[i]).start()

    produce(0, 0)
    give(0, 0)
    produce(0, 1)
    give(0, 1)

    arrived(pg_in, pg_r)
    codes = meta_in[0].reshape(256, 128)
    wanted = jnp.where(dot_nt(codes, half[k]) == slot_t[...].astype(F32), 1.0, 0.0).astype(BF)
    line = lax.broadcasted_iota(jnp.int32, (ROWS, 128), 0)
    owner = 32 * z + 2 * ((line * 2731) >> 16) + k
    values = jnp.where(
        lax.broadcasted_iota(jnp.int32, (ROWS, 128), 1) == owner, pg_in[...].reshape(ROWS, 128).astype(F32), 0.0
    ).astype(BF)
    bp_out[...] = dot(wanted, values).astype(BF).reshape(8, T, 128)

    def send_dense(s, _):
        to, core = (z + s // 2) % 4, (k + s) % 2
        remote(bp_out.at[to * 2 + core], bp_in.at[z * 2 + k], bp_s, bp_r, ident(x, y, to, core)).start()
        return 0

    lax.fori_loop(1, 8, send_dense, 0)
    pltpu.make_async_copy(bp_out.at[z * 2 + k], bp_in.at[z * 2 + k], bp_r).start()

    whole(3)
    permute(1)
    whole(1)
    whole(4)

    arrived(bp_in, bp_r)
    pick_back = jnp.sum(bp_in[...].astype(F32), axis=0)
    mixed = jnp.sum(route[0] * pick_back, axis=1, keepdims=True)
    gate_dlogit = (route[1] * (pick_back - mixed / ROUTE_SCALE)).astype(BF)
    kd_dlogit = route[2].astype(BF)

    rgs[896:, :] = jnp.zeros((8, 128), F32)
    for zq in range(4):
        mine = rows[0, :, zq * 896 : (zq + 1) * 896]
        rgs[0:896, :] = dot_tn(mine, kd_dlogit) + dot_tn(mine, gate_dlogit)
        for g in range(32):
            rgb[g % 2, zq * 16 + g // 2] = rgs[28 * g : 28 * g + 32, :].astype(BF)
    to_core = remote(rgb.at[1 - k], rk, rg_s.at[0], rg_r.at[0], ident(x, y, z, 1 - k))
    to_core.start()

    permute(2)
    whole(2)
    whole(5)
    to_core.wait_recv()
    s1[...] = (rgb[k].astype(F32) + rk[...].astype(F32)).astype(BF)

    def to_plane(d, _):
        to = (z + d) % 4
        remote(s1.at[pl.ds(to * 16, 16)], rz.at[z], rg_s.at[1], rg_r.at[1], ident(x, y, to, k)).start()
        return 0

    lax.fori_loop(1, 4, to_plane, 0)
    pltpu.make_async_copy(s1.at[pl.ds(z * 16, 16)], rz.at[z], rg_r.at[1]).start()
    extra[...] = dot_nt(kd_dlogit, router[...]) + dot_nt(gate_dlogit, router[...])
    combine(0)
    combine(3)
    combine(1)
    arrived(rz, rg_r.at[1])
    s2[...] = jnp.sum(rz[...].astype(F32), axis=0)

    def to_owner(s, _):
        dx, dy, _ = offsets(s)
        tx, ty = (x + dx) % 4, (y + dy) % 4
        remote(s2.at[tx * 4 + ty], rx.at[x * 4 + y], rg_s.at[2], rg_r.at[2], ident(tx, ty, z, k)).start()
        return 0

    lax.fori_loop(1, 16, to_owner, 0)
    pltpu.make_async_copy(s2.at[x * 4 + y], rx.at[x * 4 + y], rg_r.at[2]).start()
    combine(4)
    combine(2)
    combine(5)
    arrived(rx, rg_r.at[2])
    router_grad[...] = jnp.sum(rx[...], axis=0)[:28, :] / math.sqrt(E * T)

    for i in (0, 3, 1, 4, 2, 5):
        wide = RETURN[i][1]
        arrived(back[i], part_r.at[i])
        for q in range(2):
            cols = slice(RBASE[i] + q * wide, RBASE[i] + (q + 1) * wide)
            token_grad[:, cols] = (jnp.sum(back[i][q].astype(F32), axis=0) + extra[:, cols]).astype(BF)

    for i in range(NC):
        arrived(r1[i].at[:, pl.ds(0, 7)], r1_s.at[i])
        arrived(x2[i].at[0], x2_s.at[i])
        arrived(x2[i].at[0, pl.ds(0, 15)], x2_s.at[i])
    for i in range(NR):
        arrived(yin[i].at[pl.ds(0, 31)], y_s.at[i])
        arrived(part[i].at[pl.ds(0, 7)], part_s.at[i])
    for axis in range(3):
        arrived(meta_in.at[axis, pl.ds(0, 7)], meta_s.at[axis])
    arrived(pg_in.at[pl.ds(0, 15)], pg_s)
    arrived(bp_in.at[pl.ds(0, 7)], bp_s)
    to_core.wait_send()
    arrived(rz.at[pl.ds(0, 3)], rg_s.at[1])
    arrived(rx.at[pl.ds(0, 15)], rg_s.at[2])


def local(tokens, cotangent, router, picks, language, teacher, w_gate, w_up, w_down):
    vmem, anywhere = pl.BlockSpec(memory_space=pltpu.VMEM), pl.BlockSpec(memory_space=pl.ANY)
    buf, sem = pltpu.VMEM, pltpu.SemaphoreType.DMA
    per = lambda make, chunks=CHUNKS: tuple(buf(make(wide), BF) for _, wide in chunks)
    scratch = [
        buf((D, FF), BF), buf((D, FF), BF), buf((FF, D), BF),
        buf((2, T, D), BF),
        buf((12, T, 128), BF), buf((3, 8, T, 128), BF),
        buf((3, 768, 256), BF), buf((3, 256, 768), BF),
        per(lambda c: (2, 8, T, c)),
        per(lambda c: (32, 48, c)), per(lambda c: (2, 16, 48, c)),
        buf((ROWS, D), BF), buf((16, 24, D), BF),
        buf((3, ROWS, FF), F32), buf((ROWS, 2 * FF), BF),
        per(lambda c: (32, 24, c), RETURN),
        per(lambda c: (8, T, c), RETURN), per(lambda c: (2, 4, T, c), RETURN),
        buf((16, 24, 128), BF), buf((16, 24, 128), BF),
        buf((8, T, 128), BF), buf((8, T, 128), BF),
        buf((3, T, E), F32), buf((T, D), F32),
        buf((904, 128), F32), buf((2, 64, 32, 128), BF), buf((64, 32, 128), BF),
        buf((64, 32, 128), BF), buf((4, 16, 32, 128), BF),
        buf((16, 32, 128), F32), buf((16, 32, 128), F32),
        pltpu.SemaphoreType.REGULAR, sem((3,)), sem((3,)),
        sem((NC,)), sem((NC,)), sem((3,)), sem((3,)), sem((NC,)), sem((NC,)), sem((NR,)), sem((NR,)), sem((NR,)), sem((NR,)),
        sem, sem, sem, sem, sem((3,)), sem((3,)),
    ]
    return pl.pallas_call(
        kernel,
        out_shape=(jax.ShapeDtypeStruct((T, D), BF), jax.ShapeDtypeStruct((28, 128), F32)),
        in_specs=[anywhere, anywhere, vmem, vmem, vmem, vmem, anywhere, anywhere, anywhere, vmem, anywhere]
        + [vmem] * 5,
        out_specs=(vmem, vmem),
        scratch_shapes=scratch,
        compiler_params=pltpu.CompilerParams(
            collective_id=0, has_side_effects=True, vmem_limit_bytes=61 << 20
        ),
        cost_estimate=pl.CostEstimate(flops=15_000_000_000, bytes_accessed=24_000_000, transcendentals=400_000),
    )(tokens, cotangent, router, picks.T, language.reshape(1, T), teacher, w_gate, w_up, w_down, *tables())


def solution(mesh):
    split = P(("row", "col"), None)
    cube = P(("row", "col"), None, None)
    return jax.shard_map(
        local,
        mesh=mesh,
        in_specs=(split, split, P(), split, P(("row", "col")), P(), cube, cube, cube),
        out_specs=(split, split),
        check_vma=False,
    )
```

```python
import math

import jax
import jax.numpy as jnp
import numpy as np
from jax import lax
from jax.experimental import pallas as pl
from jax.experimental.pallas import tpu as pltpu
from jax.sharding import PartitionSpec as P

D, FF, E, T, LANGS, TOP = 3584, 1024, 128, 32, 8, 8
ROUTE_SCALE = 2.5
MESH = pl.DeviceIdType.MESH
BF, F32 = jnp.bfloat16, jnp.float32
CHUNKS = ((0, 128), (1, 128), (2, 128), (0, 384), (1, 384), (2, 256), (0, 128), (1, 128), (2, 128))
SETS = ((0, 1, 2), (3, 4, 5), (6, 7, 8))
BASE = tuple(sum(2 * c for _, c in CHUNKS[:i]) for i in range(len(CHUNKS)))
NC = len(CHUNKS)
RETURN = ((0, 128), (1, 128), (2, 128), (0, 256), (1, 256), (2, 256), (0, 256), (1, 256), (2, 128))
RBASE = tuple(sum(2 * c for _, c in RETURN[:i]) for i in range(len(RETURN)))
NR = len(RETURN)
ROWS = 384
FIRST = BASE[SETS[2][0]]
NT = (((1,), (1,)), ((), ()))
TN = (((0,), (0,)), ((), ()))


def xyz_of(axis, u, v, w):
    return ((v, w, u), (v, u, w), (u, v, w))[axis]


def uvw_of(axis, x, y, z):
    return ((z, x, y), (y, x, z), (x, y, z))[axis]


def tables():
    perm = np.zeros((2, ROWS, ROWS), np.float32)
    for x in range(4):
        for y in range(4):
            for z in range(4):
                for s in range(6):
                    row = (x * 4 + y) * 24 + z * 6 + s
                    for axis in (1, 2):
                        u, v, w = uvw_of(axis, x, y, z)
                        perm[axis - 1, row, (v * 4 + w) * 24 + u * 6 + s] = 1
    select = np.zeros((2 * E, 12 * 128), np.float32)
    for axis in range(3):
        for u in range(4):
            for v in range(4):
                for w in range(4):
                    for k in range(2):
                        x, y, z = xyz_of(axis, u, v, w)
                        expert, j = 32 * z + 8 * x + 2 * y + k, v * 8 + w * 2 + k
                        at = (axis * 4 + u) * 128
                        select[expert, at + j] = 1
                        select[E + expert, at + 32 + j] = 1
    row, lane = np.arange(768)[:, None], np.arange(128)[None, :]
    eye = np.eye(E, dtype=np.float32)
    spread = np.stack([row // 24 == lane, row // 24 + 32 == lane]).astype(np.float32)
    own, col = row % 24 // 3, np.arange(256)[None, :] // 32
    slot = np.where(own == col, row % 3 + 1, 9).astype(np.float32)
    as_bf = lambda array: jnp.asarray(array, BF)
    return (as_bf(perm), as_bf(select), as_bf(spread), as_bf(slot[:24]), as_bf(slot[:ROWS].T), as_bf(eye))


def dot(a, b):
    return jnp.dot(a, b, preferred_element_type=F32)


def dot_nt(a, b):
    return lax.dot_general(a, b, NT, preferred_element_type=F32)


def dot_tn(a, b):
    return lax.dot_general(a, b, TN, preferred_element_type=F32)


def ident(x, y, z, k):
    return (z * 2 + x // 2, (x % 2) * 8 + y * 2 + k)


def kernel(
    tokens, cotangent, router, picks, language, teacher, w_gate, w_up, w_down,
    perm, select_hbm, spread, slot, slot_t, eye,
    token_grad, router_grad,
    wg, wu, wd, rows, meta_out, meta_in, pick_l, mix_w, r1, out2, x2, xt, xc, acc, grads,
    yin, part, back, pg_out, pg_in, bp_out, bp_in, route, rgs, rgb, rk, s1, rz, rx,
    ready, w_sem, in_sem, r1_s, r1_r, meta_s, meta_r, x2_s, x2_r, y_s, y_r, part_s, part_r, pg_s, pg_r, bp_s, bp_r, rg_s, rg_r,
):
    me_row, me_col = lax.axis_index("row"), lax.axis_index("col")
    x, y, z, k = (me_row % 2) * 2 + me_col // 8, (me_col // 2) % 4, me_row // 2, me_col % 2
    places = [uvw_of(axis, x, y, z) for axis in range(3)]

    def device(axis, u, v, w, core):
        return ident(*xyz_of(axis, u, v, w), core)

    def remote(src, dst, send, recv, where):
        return pltpu.make_async_remote_copy(
            src_ref=src, dst_ref=dst, send_sem=send, recv_sem=recv, device_id=where, device_id_type=MESH
        )

    def arrived(ref, sem):
        pltpu.make_async_copy(ref, ref, sem).wait()

    weights = [
        pltpu.make_async_copy(src.at[0], dst, w_sem.at[i])
        for i, (src, dst) in enumerate(((w_gate, wg), (w_up, wu), (w_down, wd)))
    ]
    select = xt.at[0 : 2 * E, 0 : 12 * 128]
    inputs = [
        pltpu.make_async_copy(src, dst, in_sem.at[i])
        for i, (src, dst) in enumerate(((tokens, rows.at[0]), (cotangent, rows.at[1]), (select_hbm, select)))
    ]
    for copy in inputs + weights:
        copy.start()
    barrier = pltpu.get_barrier_semaphore()

    def greet(sem):
        for axis in range(3):
            u, v, w = places[axis]

            def one(s, _, axis=axis, u=u, v=v, w=w):
                where = device(axis, (u + s // 2) % 4, v, w, (k + s) % 2)
                pl.semaphore_signal(sem, inc=1, device_id=where, device_id_type=MESH)
                return 0

            lax.fori_loop(2 if axis else 1, 8, one, 0)

    greet(barrier)

    experts = lax.broadcasted_iota(jnp.int32, (E, T), 0)
    asked = jnp.zeros((E, T), F32)
    for i in range(TOP):
        asked += jnp.where(picks[i : i + 1, :] == experts, 1.0, 0.0)
    before = lax.broadcasted_iota(jnp.int32, (T, T), 0) < lax.broadcasted_iota(jnp.int32, (T, T), 1)
    rank = dot(asked.astype(BF), jnp.where(before, 1.0, 0.0).astype(BF))
    code = dot_tn((asked * (rank + 1.0)).astype(BF), eye[...])
    picked = jnp.where(code > 0.0, 1.0, 0.0)
    spoken = jnp.where(lax.broadcasted_iota(jnp.int32, (LANGS, T), 0) == language[...], 1.0, 0.0).astype(BF)
    target, left = jnp.zeros((T, E), F32), teacher[...]
    for _ in range(3):
        piece = left.astype(BF)
        left = left - piece.astype(F32)
        target += dot_tn(spoken, piece)

    for copy in inputs:
        copy.wait()
    logits = dot(rows[0], router[...])
    scores = jax.nn.sigmoid(logits)
    chosen = picked * scores
    weight = ROUTE_SCALE * chosen / jnp.sum(chosen, axis=1, keepdims=True)
    route[0] = weight
    route[1] = weight * (1.0 - scores)
    route[2] = scores - target
    told = dot(code.astype(BF), select[0:E, :]) + dot(weight.astype(BF), select[E:, :])
    for m in range(12):
        meta_out[m] = told[:, m * 128 : (m + 1) * 128].astype(BF)
    pl.semaphore_wait(barrier, 19)
    greet(ready)

    def tell(s, _):
        for axis in range(3):
            u, v, w = places[axis]
            to, core = (u + s // 2) % 4, (k + s) % 2
            remote(
                meta_out.at[axis * 4 + to], meta_in.at[axis, u * 2 + k], meta_s.at[axis], meta_r.at[axis],
                device(axis, to, v, w, core),
            ).start()
        return 0

    lax.fori_loop(1, 8, tell, 0)
    for axis in range(3):
        u = places[axis][0]
        pltpu.make_async_copy(meta_out.at[axis * 4 + u], meta_in.at[axis, u * 2 + k], meta_r.at[axis]).start()

    for chunks in SETS:

        def hop(s, _, chunks=chunks):
            for i in chunks:
                axis, wide = CHUNKS[i]
                u, v, w = places[axis]
                core = (k + s) % 2
                start = pl.multiple_of(BASE[i] + core * wide, 128)
                remote(
                    rows.at[:, :, pl.ds(start, wide)], r1[i].at[:, u * 2 + k], r1_s.at[i], r1_r.at[i],
                    device(axis, (u + s // 2) % 4, v, w, core),
                ).start()
            return 0

        lax.fori_loop(1, 8, hop, 0)
        for i in chunks:
            axis, wide = CHUNKS[i]
            start = pl.multiple_of(BASE[i] + k * wide, 128)
            into = r1[i].at[:, places[axis][0] * 2 + k]
            pltpu.make_async_copy(rows.at[:, :, pl.ds(start, wide)], into, r1_r.at[i]).start()

    def offsets(s):
        j = s % 16
        return j % 4, (j // 4 + j) % 4, s // 16

    for axis in range(3):
        arrived(meta_in.at[axis], meta_r.at[axis])
        codes = meta_in[axis].reshape(256, 128)
        slots = jnp.broadcast_to(slot[...].astype(F32)[None], (32, 24, 256)).reshape(768, 256)
        pick_l[axis] = jnp.where(dot_nt(spread[0], codes) == slots, 1.0, 0.0).astype(BF)

    def relay(chunks):
        for i in chunks:
            axis, wide = CHUNKS[i]
            arrived(r1[i], r1_r.at[i])

            def gather(g, _, i=i, axis=axis, wide=wide):
                lhs = pick_l[axis, pl.ds(pl.multiple_of(g * 192, 192), 192), :]
                for a in range(2):
                    got = dot(lhs, r1[i][a].reshape(256, wide)).astype(BF)
                    out2[i][pl.ds(g * 8, 8), a * 24 : a * 24 + 24, :] = got.reshape(8, 24, wide)
                return 0

            lax.fori_loop(0, 4, gather, 0)

        if chunks == SETS[0]:
            pl.semaphore_wait(ready, 19)

        def spread_out(s, _):
            dv, dw, dk = offsets(s)
            for i in chunks:
                axis, wide = CHUNKS[i]
                u, v, w = places[axis]
                tv, tw, core = (v + dv) % 4, (w + dw) % 4, (k + dk) % 2
                remote(
                    out2[i].at[tv * 8 + tw * 2 + core], x2[i].at[k, v * 4 + w], x2_s.at[i], x2_r.at[i],
                    device(axis, u, tv, tw, core),
                ).start()
            return 0

        lax.fori_loop(1, 32, spread_out, 0)
        for i in chunks:
            u, v, w = places[CHUNKS[i][0]]
            pltpu.make_async_copy(out2[i].at[v * 8 + w * 2 + k], x2[i].at[k, v * 4 + w], x2_r.at[i]).start()

    for chunks in SETS:
        relay(chunks)

    slots_t = jnp.concatenate([slot_t[...].astype(F32)] * 2, axis=1)
    for axis in range(3):
        codes = meta_in[axis].reshape(256, 128)
        mix_w[axis] = jnp.where(dot_nt(codes, spread[0]) == slots_t, dot_nt(codes, spread[1]), 0.0).astype(BF)

    def collect(chunks):
        for i in chunks:
            axis, wide = CHUNKS[i]
            arrived(x2[i], x2_r.at[i])
            for q in range(2):
                cols = slice(BASE[i] + q * wide, BASE[i] + (q + 1) * wide)
                for a in range(2):
                    got = x2[i][q, :, a * 24 : a * 24 + 24, :].reshape(ROWS, wide)
                    got = got if axis == 0 else dot(perm[axis - 1], got).astype(BF)
                    if a == 0:
                        xt[:, cols] = got
                    else:
                        xc[:, :, cols] = got.reshape(16, 24, wide)

    def parts(n, low, high):
        cols = pl.ds(pl.multiple_of(n * 256, 256), 256)
        gate = dot(xt[:, low:high], wg[low:high, cols])
        up = dot(xt[:, low:high], wu[low:high, cols])
        into = dot_nt(xc[:, :, low:high].reshape(ROWS, high - low), wd[cols, low:high])
        return cols, gate, up, into

    def first(n, _):
        cols, *values = parts(n, 0, FIRST)
        for i, value in enumerate(values):
            acc[i, :, cols] = value
        return 0

    def second(n, total):
        cols, gate, up, into = parts(n, FIRST, D)
        gate, up, into = acc[0, :, cols] + gate, acc[1, :, cols] + up, acc[2, :, cols] + into
        sigma = jax.nn.sigmoid(gate)
        active = gate * sigma
        up_part = into * active
        grads[:, cols] = (into * up * (sigma * (1.0 + gate * (1.0 - sigma)))).astype(BF)
        grads[:, pl.ds(pl.multiple_of(FF + n * 256, 256), 256)] = up_part.astype(BF)
        return total + jnp.sum(up_part * up, axis=1, keepdims=True)

    collect(SETS[0])
    collect(SETS[1])
    for copy in weights:
        copy.wait()
    lax.fori_loop(0, FF // 256, first, 0)
    collect(SETS[2])
    pick_grad = lax.fori_loop(0, FF // 256, second, jnp.zeros((ROWS, 1), F32))
    pg_out[...] = jnp.broadcast_to(pick_grad, (ROWS, 128)).astype(BF).reshape(16, 24, 128)

    def send_pick(s, _):
        dv, dw, _ = offsets(s)
        tx, ty = (x + dv) % 4, (y + dw) % 4
        remote(pg_out.at[tx * 4 + ty], pg_in.at[x * 4 + y], pg_s, pg_r, ident(tx, ty, z, k)).start()
        return 0

    lax.fori_loop(1, 16, send_pick, 0)
    pltpu.make_async_copy(pg_out.at[x * 4 + y], pg_in.at[x * 4 + y], pg_r).start()

    def permute(axis):
        if axis:
            xt[:, (axis - 1) * 2 * FF : axis * 2 * FF] = dot_tn(perm[axis - 1], grads[...]).astype(BF)

    def produce(i, dq):
        axis, wide = RETURN[i]
        cols = pl.ds(pl.multiple_of(RBASE[i] + (k + dq) % 2 * wide, 128), wide)
        lhs = xt.at[:, (axis - 1) * 2 * FF : axis * 2 * FF] if axis else grads
        got = dot_nt(lhs[:, :FF], wg[cols, :]) + dot_nt(lhs[:, FF:], wu[cols, :])
        xc[:, :, cols] = got.astype(BF).reshape(16, 24, wide)

    def give(chunks):
        def one(s, _):
            dv, dw, dk = offsets(s)
            for i in chunks:
                axis, wide = RETURN[i]
                u, v, w = places[axis]
                tv, tw, q = (v + dv) % 4, (w + dw) % 4, (k + dk) % 2
                cols = pl.ds(pl.multiple_of(RBASE[i] + q * wide, 128), wide)
                remote(
                    xc.at[tv * 4 + tw, :, cols], yin[i].at[v * 8 + w * 2 + k], y_s.at[i], y_r.at[i],
                    device(axis, u, tv, tw, q),
                ).start()
            return 0

        lax.fori_loop(1, 32, one, 0)
        for i in chunks:
            axis, wide = RETURN[i]
            u, v, w = places[axis]
            cols = pl.ds(pl.multiple_of(RBASE[i] + k * wide, 128), wide)
            pltpu.make_async_copy(xc.at[v * 4 + w, :, cols], yin[i].at[v * 8 + w * 2 + k], y_r.at[i]).start()

    def extra(start, wide):
        return acc.at[0, start // FF * T : start // FF * T + T, start % FF : start % FF + wide]

    def share(i):
        return acc.at[1, pl.ds(pl.multiple_of(i // 8 * 32, 32), 32), pl.ds(pl.multiple_of(i % 8 * 128, 128), 128)]

    def combine(i):
        axis, wide = RETURN[i]
        u, v, w = places[axis]
        arrived(yin[i], y_r.at[i])
        part[i][...] = dot(mix_w[axis], yin[i][...].reshape(768, wide)).astype(BF).reshape(8, T, wide)

        def give_back(s, _):
            to, core = (u + s // 2) % 4, (k + s) % 2
            remote(
                part[i].at[to * 2 + core], back[i].at[k, u], part_s.at[i], part_r.at[i], device(axis, to, v, w, core)
            ).start()
            return 0

        lax.fori_loop(1, 8, give_back, 0)
        pltpu.make_async_copy(part[i].at[u * 2 + k], back[i].at[k, u], part_r.at[i]).start()

    for axis in range(2):
        permute(axis)
        for dq in range(2):
            produce(axis, dq)
        give((axis,))

    arrived(pg_in, pg_r)
    codes = meta_in[0].reshape(256, 128)
    line, lane = (lax.broadcasted_iota(jnp.int32, (ROWS, 128), dim) for dim in (0, 1))
    owner = 2 * ((line * 2731) >> 16) + k
    one_of = jnp.where(lane == owner, 1.0, 0.0).astype(BF)
    wanted = jnp.where(dot_nt(codes, one_of) == slot_t[...].astype(F32), 1.0, 0.0).astype(BF)
    values = jnp.where(lane == 32 * z + owner, pg_in[...].reshape(ROWS, 128).astype(F32), 0.0).astype(BF)
    bp_out[...] = dot(wanted, values).astype(BF).reshape(8, T, 128)

    def send_dense(s, _):
        to, core = (z + s // 2) % 4, (k + s) % 2
        remote(bp_out.at[to * 2 + core], bp_in.at[z * 2 + k], bp_s, bp_r, ident(x, y, to, core)).start()
        return 0

    lax.fori_loop(1, 8, send_dense, 0)
    pltpu.make_async_copy(bp_out.at[z * 2 + k], bp_in.at[z * 2 + k], bp_r).start()

    permute(2)
    for dq in range(2):
        produce(2, dq)
    give((2,))
    for i in SETS[1]:
        for dq in range(2):
            produce(i, dq)
    give(SETS[1])

    arrived(bp_in, bp_r)
    pick_back = jnp.sum(bp_in[...].astype(F32), axis=0)
    mixed = jnp.sum(route[0] * pick_back, axis=1, keepdims=True)
    gate_dlogit = (route[1] * (pick_back - mixed / ROUTE_SCALE)).astype(BF)
    kd_dlogit = route[2].astype(BF)

    rgs[896:, :] = jnp.zeros((8, 128), F32)
    for zq in range(4):
        mine = rows[0, :, zq * 896 : (zq + 1) * 896]
        rgs[0:896, :] = dot_tn(mine, kd_dlogit) + dot_tn(mine, gate_dlogit)
        for g in range(32):
            rgb[g % 2, zq * 16 + g // 2] = rgs[28 * g : 28 * g + 32, :].astype(BF)
    to_core = remote(rgb.at[1 - k], rk, rg_s.at[0], rg_r.at[0], ident(x, y, z, 1 - k))
    to_core.start()

    for i in SETS[2]:
        for dq in range(2):
            produce(i, dq)
    to_core.wait_recv()
    s1[...] = (rgb[k].astype(F32) + rk[...].astype(F32)).astype(BF)

    def to_plane(d, _):
        to = (z + d) % 4
        remote(s1.at[pl.ds(to * 16, 16)], rz.at[z], rg_s.at[1], rg_r.at[1], ident(x, y, to, k)).start()
        return 0

    lax.fori_loop(1, 4, to_plane, 0)
    pltpu.make_async_copy(s1.at[pl.ds(z * 16, 16)], rz.at[z], rg_r.at[1]).start()
    give(SETS[2])
    for j in range(7):
        cols = slice(j * 512, j * 512 + 512)
        extra(j * 512, 512)[...] = dot_nt(kd_dlogit, router[cols, :]) + dot_nt(gate_dlogit, router[cols, :])
    for i in SETS[0] + SETS[1]:
        combine(i)
    arrived(rz, rg_r.at[1])
    for i in range(16):
        share(i)[...] = jnp.sum(rz[:, i].astype(F32), axis=0)

    def to_owner(s, _):
        dx, dy, _ = offsets(s)
        tx, ty = (x + dx) % 4, (y + dy) % 4
        remote(share(tx * 4 + ty), rx.at[x * 4 + y], rg_s.at[2], rg_r.at[2], ident(tx, ty, z, k)).start()
        return 0

    lax.fori_loop(1, 16, to_owner, 0)
    pltpu.make_async_copy(share(x * 4 + y), rx.at[x * 4 + y], rg_r.at[2]).start()
    for i in SETS[2]:
        combine(i)
    arrived(rx, rg_r.at[2])
    router_grad[...] = jnp.sum(rx[...], axis=0)[:28, :] / math.sqrt(E * T)

    for i in range(NR):
        wide = RETURN[i][1]
        arrived(back[i], part_r.at[i])
        for q in range(2):
            start = RBASE[i] + q * wide
            total = jnp.sum(back[i][q].astype(F32), axis=0) + extra(start, wide)[...]
            token_grad[:, start : start + wide] = total.astype(BF)

    for i in range(NC):
        arrived(r1[i].at[:, pl.ds(0, 7)], r1_s.at[i])
        arrived(x2[i].at[0], x2_s.at[i])
        arrived(x2[i].at[0, pl.ds(0, 15)], x2_s.at[i])
    for i in range(NR):
        arrived(yin[i].at[pl.ds(0, 31)], y_s.at[i])
        arrived(part[i].at[pl.ds(0, 7)], part_s.at[i])
    for axis in range(3):
        arrived(meta_in.at[axis, pl.ds(0, 7)], meta_s.at[axis])
    arrived(pg_in.at[pl.ds(0, 15)], pg_s)
    arrived(bp_in.at[pl.ds(0, 7)], bp_s)
    to_core.wait_send()
    arrived(rz.at[pl.ds(0, 3)], rg_s.at[1])
    arrived(rx.at[pl.ds(0, 15)], rg_s.at[2])


def local(tokens, cotangent, router, picks, language, teacher, w_gate, w_up, w_down):
    vmem, anywhere = pl.BlockSpec(memory_space=pltpu.VMEM), pl.BlockSpec(memory_space=pl.ANY)
    buf, sem = pltpu.VMEM, pltpu.SemaphoreType.DMA
    per = lambda make, chunks=CHUNKS: tuple(buf(make(wide), BF) for _, wide in chunks)
    scratch = [
        buf((D, FF), BF), buf((D, FF), BF), buf((FF, D), BF),
        buf((2, T, D), BF),
        buf((12, T, 128), BF), buf((3, 8, T, 128), BF),
        buf((3, 768, 256), BF), buf((3, 256, 768), BF),
        per(lambda c: (2, 8, T, c)),
        per(lambda c: (32, 48, c)), per(lambda c: (2, 16, 48, c)),
        buf((ROWS, 4 * FF), BF), buf((16, 24, D), BF),
        buf((3, ROWS, FF), F32), buf((ROWS, 2 * FF), BF),
        per(lambda c: (32, 24, c), RETURN),
        per(lambda c: (8, T, c), RETURN), per(lambda c: (2, 4, T, c), RETURN),
        buf((16, 24, 128), BF), buf((16, 24, 128), BF),
        buf((8, T, 128), BF), buf((8, T, 128), BF),
        buf((3, T, E), F32),
        buf((904, 128), F32), buf((2, 64, 32, 128), BF), buf((64, 32, 128), BF),
        buf((64, 32, 128), BF), buf((4, 16, 32, 128), BF),
        buf((16, 32, 128), F32),
        pltpu.SemaphoreType.REGULAR, sem((3,)), sem((3,)),
        sem((NC,)), sem((NC,)), sem((3,)), sem((3,)), sem((NC,)), sem((NC,)), sem((NR,)), sem((NR,)), sem((NR,)), sem((NR,)),
        sem, sem, sem, sem, sem((3,)), sem((3,)),
    ]
    return pl.pallas_call(
        kernel,
        out_shape=(jax.ShapeDtypeStruct((T, D), BF), jax.ShapeDtypeStruct((28, 128), F32)),
        in_specs=[anywhere, anywhere, vmem, vmem, vmem, vmem, anywhere, anywhere, anywhere, vmem, anywhere]
        + [vmem] * 4,
        out_specs=(vmem, vmem),
        scratch_shapes=scratch,
        compiler_params=pltpu.CompilerParams(
            collective_id=0, has_side_effects=True, vmem_limit_bytes=61 << 20
        ),
        cost_estimate=pl.CostEstimate(flops=15_000_000_000, bytes_accessed=24_000_000, transcendentals=400_000),
    )(tokens, cotangent, router, picks.T, language.reshape(1, T), teacher, w_gate, w_up, w_down, *tables())


def solution(mesh):
    split = P(("row", "col"), None)
    cube = P(("row", "col"), None, None)
    return jax.shard_map(
        local,
        mesh=mesh,
        in_specs=(split, split, P(), split, P(("row", "col")), P(), cube, cube, cube),
        out_specs=(split, split),
        check_vma=False,
    )
```

```python
import math

import jax
import jax.numpy as jnp
import numpy as np
from jax import lax
from jax.experimental import pallas as pl
from jax.experimental.pallas import tpu as pltpu
from jax.sharding import PartitionSpec as P

D, FF, E, T, LANGS, TOP = 3584, 1024, 128, 32, 8, 8
ROUTE_SCALE = 2.5
MESH = pl.DeviceIdType.MESH
BF, F32 = jnp.bfloat16, jnp.float32
Z, Y, X = (0, 0), (1, 1), (2, 2)
CHUNKS = ((Z, 128), (Y, 128), (X, 128), (Z, 384), (Y, 256), (X, 256), ((1, 2), 128), (Z, 128), (Y, 128), (X, 128))
SETS = ((0, 1, 2), (3, 4, 5, 6), (7, 8, 9))
BASE = tuple(sum(2 * c for _, c in CHUNKS[:i]) for i in range(len(CHUNKS)))
NC = len(CHUNKS)
RETURN = ((Z, 128), (Y, 128), (X, 128), (Z, 256), (Y, 256), (X, 256), (Z, 256), (Y, 128), (X, 128), (Z, 128))
RSETS = ((0, 1, 2), (3, 4, 5), (6, 7, 8, 9))
RBASE = tuple(sum(2 * c for _, c in RETURN[:i]) for i in range(len(RETURN)))
NR = len(RETURN)
ROWS = 384
FIRST = BASE[SETS[2][0]]
NT = (((1,), (1,)), ((), ()))
TN = (((0,), (0,)), ((), ()))


def xyz_of(axis, u, v, w):
    return ((v, w, u), (v, u, w), (u, v, w))[axis]


def uvw_of(axis, x, y, z):
    return ((z, x, y), (y, x, z), (x, y, z))[axis]


def tables():
    perm = np.zeros((2, ROWS, ROWS), np.float32)
    for x in range(4):
        for y in range(4):
            for z in range(4):
                for s in range(6):
                    row = (x * 4 + y) * 24 + z * 6 + s
                    for axis in (1, 2):
                        u, v, w = uvw_of(axis, x, y, z)
                        perm[axis - 1, row, (v * 4 + w) * 24 + u * 6 + s] = 1
    select = np.zeros((2 * E, 12 * 128), np.float32)
    for axis in range(3):
        for u in range(4):
            for v in range(4):
                for w in range(4):
                    for k in range(2):
                        x, y, z = xyz_of(axis, u, v, w)
                        expert, j = 32 * z + 8 * x + 2 * y + k, v * 8 + w * 2 + k
                        at = (axis * 4 + u) * 128
                        select[expert, at + j] = 1
                        select[E + expert, at + 32 + j] = 1
    row, lane = np.arange(768)[:, None], np.arange(128)[None, :]
    eye = np.eye(E, dtype=np.float32)
    spread = np.stack([row // 24 == lane, row // 24 + 32 == lane]).astype(np.float32)
    own, col = row % 24 // 3, np.arange(256)[None, :] // 32
    slot = np.where(own == col, row % 3 + 1, 9).astype(np.float32)
    as_bf = lambda array: jnp.asarray(array, BF)
    return (as_bf(perm), as_bf(select), as_bf(spread), as_bf(slot[:24]), as_bf(slot[:ROWS].T), as_bf(eye))


def dot(a, b):
    return jnp.dot(a, b, preferred_element_type=F32)


def dot_nt(a, b):
    return lax.dot_general(a, b, NT, preferred_element_type=F32)


def dot_tn(a, b):
    return lax.dot_general(a, b, TN, preferred_element_type=F32)


def ident(x, y, z, k):
    return (z * 2 + x // 2, (x % 2) * 8 + y * 2 + k)


def kernel(
    tokens, cotangent, router, picks, language, teacher, w_gate, w_up, w_down,
    perm, select_hbm, spread, slot, slot_t, eye,
    token_grad, router_grad,
    wg, wu, wd, rows, meta_out, meta_in, pick_l, mix_w, r1, out2, x2, xt, xc, acc, grads,
    yin, part, back, pg_out, pg_in, bp_out, bp_in, route, rgs, rgb, rk, s1, rz, rx,
    ready, w_sem, in_sem, r1_s, r1_r, meta_s, meta_r, share_s, share_r, x2_s, x2_r, y_s, y_r, part_s, part_r, pg_s, pg_r, bp_s, bp_r, rg_s, rg_r,
):
    me_row, me_col = lax.axis_index("row"), lax.axis_index("col")
    x, y, z, k = (me_row % 2) * 2 + me_col // 8, (me_col // 2) % 4, me_row // 2, me_col % 2
    places = [uvw_of(axis, x, y, z) for axis in range(3)]

    def by_core(values, core):
        return values[0] + core * (values[1] - values[0])

    def spot(axes, relay):
        if axes[0] == axes[1]:
            return places[axes[0]]
        return tuple(by_core(pair, relay) for pair in zip(places[axes[0]], places[axes[1]]))

    def device(axes, relay, u, v, w, core):
        first, second = (xyz_of(axis, u, v, w) for axis in axes)
        if axes[0] == axes[1]:
            return ident(*first, core)
        return ident(*(by_core(pair, relay) for pair in zip(first, second)), core)

    def axis_of(axes, relay):
        return axes[0] if axes[0] == axes[1] else by_core(axes, relay)

    def remote(src, dst, send, recv, where):
        return pltpu.make_async_remote_copy(
            src_ref=src, dst_ref=dst, send_sem=send, recv_sem=recv, device_id=where, device_id_type=MESH
        )

    def arrived(ref, sem):
        pltpu.make_async_copy(ref, ref, sem).wait()

    weights = [
        pltpu.make_async_copy(src.at[0], dst, w_sem.at[i])
        for i, (src, dst) in enumerate(((w_gate, wg), (w_up, wu), (w_down, wd)))
    ]
    select = xt.at[0 : 2 * E, 0 : 12 * 128]
    inputs = [
        pltpu.make_async_copy(src, dst, in_sem.at[i])
        for i, (src, dst) in enumerate(((tokens, rows.at[0]), (cotangent, rows.at[1]), (select_hbm, select)))
    ]
    for copy in inputs + weights:
        copy.start()
    barrier = pltpu.get_barrier_semaphore()

    def greet(sem):
        for axis in range(3):
            u, v, w = places[axis]

            def one(s, _, axis=axis, u=u, v=v, w=w):
                where = device((axis, axis), 0, (u + s // 2) % 4, v, w, (k + s) % 2)
                pl.semaphore_signal(sem, inc=1, device_id=where, device_id_type=MESH)
                return 0

            lax.fori_loop(2 if axis else 1, 8, one, 0)

    greet(barrier)

    experts = lax.broadcasted_iota(jnp.int32, (E, T), 0)
    asked = jnp.zeros((E, T), F32)
    for i in range(TOP):
        asked += jnp.where(picks[i : i + 1, :] == experts, 1.0, 0.0)
    before = lax.broadcasted_iota(jnp.int32, (T, T), 0) < lax.broadcasted_iota(jnp.int32, (T, T), 1)
    rank = dot(asked.astype(BF), jnp.where(before, 1.0, 0.0).astype(BF))
    code = dot_tn((asked * (rank + 1.0)).astype(BF), eye[...])
    picked = jnp.where(code > 0.0, 1.0, 0.0)
    inputs[2].wait()
    told = dot(code.astype(BF), select[0:E, :])
    for m in range(12):
        meta_out[m] = told[:, m * 128 : (m + 1) * 128].astype(BF)
    spoken = jnp.where(lax.broadcasted_iota(jnp.int32, (LANGS, T), 0) == language[...], 1.0, 0.0).astype(BF)
    target, left = jnp.zeros((T, E), F32), teacher[...]
    for _ in range(3):
        piece = left.astype(BF)
        left = left - piece.astype(F32)
        target += dot_tn(spoken, piece)

    pl.semaphore_wait(barrier, 19)
    greet(ready)

    def tell(source, into, send, recv):
        def one(s, _):
            for axis in range(3):
                u, v, w = places[axis]
                to, core = (u + s // 2) % 4, (k + s) % 2
                remote(
                    source.at[axis * 4 + to], into.at[axis * 8 + u * 2 + k], send.at[axis], recv.at[axis],
                    device((axis, axis), 0, to, v, w, core),
                ).start()
            return 0

        lax.fori_loop(1, 8, one, 0)
        for axis in range(3):
            u = places[axis][0]
            pltpu.make_async_copy(source.at[axis * 4 + u], into.at[axis * 8 + u * 2 + k], recv.at[axis]).start()

    share_out, share_in = rgb.at[0], rk

    def send_rows(chunks):
        def hop(s, _):
            core = (k + s) % 2
            for i in chunks:
                axes, wide = CHUNKS[i]
                u, v, w = spot(axes, core)
                start = pl.multiple_of(BASE[i] + core * wide, 128)
                remote(
                    rows.at[:, :, pl.ds(start, wide)], r1[i].at[:, u * 2 + k], r1_s.at[i], r1_r.at[i],
                    device(axes, core, (u + s // 2) % 4, v, w, core),
                ).start()
            return 0

        lax.fori_loop(1, 8, hop, 0)
        for i in chunks:
            axes, wide = CHUNKS[i]
            start = pl.multiple_of(BASE[i] + k * wide, 128)
            into = r1[i].at[:, spot(axes, k)[0] * 2 + k]
            pltpu.make_async_copy(rows.at[:, :, pl.ds(start, wide)], into, r1_r.at[i]).start()

    tell(meta_out, meta_in, meta_s, meta_r)
    for copy in inputs[:2]:
        copy.wait()
    for chunks in SETS:
        send_rows(chunks)

    logits = dot(rows[0], router[...])
    scores = jax.nn.sigmoid(logits)
    chosen = picked * scores
    weight = ROUTE_SCALE * chosen / jnp.sum(chosen, axis=1, keepdims=True)
    route[0] = weight
    route[1] = weight * (1.0 - scores)
    route[2] = scores - target
    told = dot(weight.astype(BF), select[E:, :])
    for m in range(12):
        share_out.at[m][...] = told[:, m * 128 : (m + 1) * 128].astype(BF)

    tell(share_out, share_in, share_s, share_r)

    def offsets(s):
        j = s % 16
        return j % 4, (j // 4 + j) % 4, s // 16

    for axis in range(3):
        arrived(meta_in.at[axis * 8 : axis * 8 + 8], meta_r.at[axis])
        codes = meta_in[axis * 8 : axis * 8 + 8].reshape(256, 128)
        slots = jnp.broadcast_to(slot[...].astype(F32)[None], (32, 24, 256)).reshape(768, 256)
        pick_l[axis] = jnp.where(dot_nt(spread[0], codes) == slots, 1.0, 0.0).astype(BF)

    def relay(chunks):
        for i in chunks:
            axes, wide = CHUNKS[i]
            arrived(r1[i], r1_r.at[i])

            def gather(g, _, i=i, axes=axes, wide=wide):
                lhs = pick_l[axis_of(axes, k), pl.ds(pl.multiple_of(g * 192, 192), 192), :]
                for a in range(2):
                    got = dot(lhs, r1[i][a].reshape(256, wide)).astype(BF)
                    out2[i][pl.ds(g * 8, 8), a * 24 : a * 24 + 24, :] = got.reshape(8, 24, wide)
                return 0

            lax.fori_loop(0, 4, gather, 0)

        if chunks == SETS[0]:
            pl.semaphore_wait(ready, 19)

        def spread_out(s, _):
            dv, dw, dk = offsets(s)
            for i in chunks:
                axes, wide = CHUNKS[i]
                u, v, w = spot(axes, k)
                tv, tw, core = (v + dv) % 4, (w + dw) % 4, (k + dk) % 2
                remote(
                    out2[i].at[tv * 8 + tw * 2 + core], x2[i].at[k, v * 4 + w], x2_s.at[i], x2_r.at[i],
                    device(axes, k, u, tv, tw, core),
                ).start()
            return 0

        lax.fori_loop(1, 32, spread_out, 0)
        for i in chunks:
            u, v, w = spot(CHUNKS[i][0], k)
            pltpu.make_async_copy(out2[i].at[v * 8 + w * 2 + k], x2[i].at[k, v * 4 + w], x2_r.at[i]).start()

    for chunks in SETS:
        relay(chunks)

    slots_t = jnp.concatenate([slot_t[...].astype(F32)] * 2, axis=1)
    for axis in range(3):
        arrived(share_in.at[axis * 8 : axis * 8 + 8], share_r.at[axis])
        codes, shares = (ref[axis * 8 : axis * 8 + 8].reshape(256, 128) for ref in (meta_in, share_in))
        mix_w[axis] = jnp.where(dot_nt(codes, spread[0]) == slots_t, dot_nt(shares, spread[1]), 0.0).astype(BF)

    def collect(chunks):
        for i in chunks:
            axes, wide = CHUNKS[i]
            arrived(x2[i], x2_r.at[i])
            taken = [(q, a) for q in range(2) for a in range(2)]
            every = [x2[i][q, :, a * 24 : a * 24 + 24, :].reshape(ROWS, wide) for q, a in taken]
            step = 4 if axes[0] == axes[1] and wide == 128 else 2
            for n in range(0, 4, step):
                axis = axes[taken[n][0]]
                some = every[n : n + step]
                if axis:
                    moved = dot(perm[axis - 1], jnp.concatenate(some, axis=1)).astype(BF)
                    some = [moved[:, j * wide : (j + 1) * wide] for j in range(step)]
                for (q, a), got in zip(taken[n : n + step], some):
                    cols = slice(BASE[i] + q * wide, BASE[i] + (q + 1) * wide)
                    if a == 0:
                        xt[:, cols] = got
                    else:
                        xc[:, :, cols] = got.reshape(16, 24, wide)

    def parts(n, low, high):
        cols = pl.ds(pl.multiple_of(n * 256, 256), 256)
        gate = dot(xt[:, low:high], wg[low:high, cols])
        up = dot(xt[:, low:high], wu[low:high, cols])
        into = dot_nt(xc[:, :, low:high].reshape(ROWS, high - low), wd[cols, low:high])
        return cols, gate, up, into

    def first(n, _):
        cols, *values = parts(n, 0, FIRST)
        for i, value in enumerate(values):
            acc[i, :, cols] = value
        return 0

    def second(n, total):
        cols, gate, up, into = parts(n, FIRST, D)
        gate, up, into = acc[0, :, cols] + gate, acc[1, :, cols] + up, acc[2, :, cols] + into
        sigma = jax.nn.sigmoid(gate)
        active = gate * sigma
        up_part = into * active
        grads[:, cols] = (into * up * (sigma * (1.0 + gate * (1.0 - sigma)))).astype(BF)
        grads[:, pl.ds(pl.multiple_of(FF + n * 256, 256), 256)] = up_part.astype(BF)
        return total + jnp.sum(up_part * up, axis=1, keepdims=True)

    collect(SETS[0])
    collect(SETS[1])
    for copy in weights:
        copy.wait()
    lax.fori_loop(0, FF // 256, first, 0)
    collect(SETS[2])
    pick_grad = lax.fori_loop(0, FF // 256, second, jnp.zeros((ROWS, 1), F32))
    pg_out[...] = jnp.broadcast_to(pick_grad, (ROWS, 128)).astype(BF).reshape(16, 24, 128)

    def send_pick(s, _):
        dv, dw, _ = offsets(s)
        tx, ty = (x + dv) % 4, (y + dw) % 4
        remote(pg_out.at[tx * 4 + ty], pg_in.at[x * 4 + y], pg_s, pg_r, ident(tx, ty, z, k)).start()
        return 0

    lax.fori_loop(1, 16, send_pick, 0)
    pltpu.make_async_copy(pg_out.at[x * 4 + y], pg_in.at[x * 4 + y], pg_r).start()

    def permute(axis):
        if axis:
            xt[:, (axis - 1) * 2 * FF : axis * 2 * FF] = dot_tn(perm[axis - 1], grads[...]).astype(BF)

    def produce(i, dq):
        axes, wide = RETURN[i]
        q = (k + dq) % 2
        cols = pl.ds(pl.multiple_of(RBASE[i] + q * wide, 128), wide)
        if axes == Z:
            lhs = grads
        elif axes[0] == axes[1]:
            lhs = xt.at[:, (axes[0] - 1) * 2 * FF : axes[0] * 2 * FF]
        else:
            lhs = xt.at[:, pl.ds(pl.multiple_of((axis_of(axes, q) - 1) * 2 * FF, 128), 2 * FF)]
        got = dot_nt(lhs[:, :FF], wg[cols, :]) + dot_nt(lhs[:, FF:], wu[cols, :])
        xc[:, :, cols] = got.astype(BF).reshape(16, 24, wide)

    def give(chunks):
        def one(s, _):
            dv, dw, dk = offsets(s)
            for i in chunks:
                axes, wide = RETURN[i]
                q = (k + dk) % 2
                u, v, w = spot(axes, q)
                tv, tw = (v + dv) % 4, (w + dw) % 4
                cols = pl.ds(pl.multiple_of(RBASE[i] + q * wide, 128), wide)
                remote(
                    xc.at[tv * 4 + tw, :, cols], yin[i].at[v * 8 + w * 2 + k], y_s.at[i], y_r.at[i],
                    device(axes, q, u, tv, tw, q),
                ).start()
            return 0

        lax.fori_loop(1, 32, one, 0)
        for i in chunks:
            axes, wide = RETURN[i]
            u, v, w = spot(axes, k)
            cols = pl.ds(pl.multiple_of(RBASE[i] + k * wide, 128), wide)
            pltpu.make_async_copy(xc.at[v * 4 + w, :, cols], yin[i].at[v * 8 + w * 2 + k], y_r.at[i]).start()

    def extra(start, wide):
        return acc.at[0, start // FF * T : start // FF * T + T, start % FF : start % FF + wide]

    def combine(i):
        axes, wide = RETURN[i]
        u, v, w = spot(axes, k)
        arrived(yin[i], y_r.at[i])
        part[i][...] = dot(mix_w[axis_of(axes, k)], yin[i][...].reshape(768, wide)).astype(BF).reshape(8, T, wide)

        def give_back(s, _):
            to, core = (u + s // 2) % 4, (k + s) % 2
            remote(
                part[i].at[to * 2 + core], back[i].at[k, u], part_s.at[i], part_r.at[i], device(axes, k, to, v, w, core)
            ).start()
            return 0

        lax.fori_loop(1, 8, give_back, 0)
        pltpu.make_async_copy(part[i].at[u * 2 + k], back[i].at[k, u], part_r.at[i]).start()

    for axis in range(2):
        permute(axis)
        for dq in range(2):
            produce(axis, dq)
        give((axis,))

    arrived(pg_in, pg_r)
    codes = meta_in[0:8].reshape(256, 128)
    line, lane = (lax.broadcasted_iota(jnp.int32, (ROWS, 128), dim) for dim in (0, 1))
    owner = 2 * ((line * 2731) >> 16) + k
    one_of = jnp.where(lane == owner, 1.0, 0.0).astype(BF)
    wanted = jnp.where(dot_nt(codes, one_of) == slot_t[...].astype(F32), 1.0, 0.0).astype(BF)
    values = jnp.where(lane == 32 * z + owner, pg_in[...].reshape(ROWS, 128).astype(F32), 0.0).astype(BF)
    bp_out[...] = dot(wanted, values).astype(BF).reshape(8, T, 128)

    def send_dense(s, _):
        to, core = (z + s // 2) % 4, (k + s) % 2
        remote(bp_out.at[to * 2 + core], bp_in.at[z * 2 + k], bp_s, bp_r, ident(x, y, to, core)).start()
        return 0

    lax.fori_loop(1, 8, send_dense, 0)
    pltpu.make_async_copy(bp_out.at[z * 2 + k], bp_in.at[z * 2 + k], bp_r).start()

    permute(2)
    for dq in range(2):
        produce(2, dq)
    give((2,))
    for i in RSETS[1]:
        for dq in range(2):
            produce(i, dq)
    give(RSETS[1])

    arrived(bp_in, bp_r)
    pick_back = jnp.sum(bp_in[...].astype(F32), axis=0)
    mixed = jnp.sum(route[0] * pick_back, axis=1, keepdims=True)
    gate_dlogit = (route[1] * (pick_back - mixed / ROUTE_SCALE)).astype(BF)
    kd_dlogit = route[2].astype(BF)

    for axis in range(3):
        arrived(share_in.at[0:7], share_s.at[axis])
    rgs[896:, :] = jnp.zeros((8, 128), F32)
    for zq in range(4):
        mine = rows[0, :, zq * 896 : (zq + 1) * 896]
        rgs[0:896, :] = dot_tn(mine, kd_dlogit) + dot_tn(mine, gate_dlogit)
        for g in range(32):
            rgb[g % 2, zq * 16 + g // 2] = rgs[28 * g : 28 * g + 32, :].astype(BF)
    to_core = remote(rgb.at[1 - k], rk, rg_s.at[0], rg_r.at[0], ident(x, y, z, 1 - k))
    to_core.start()

    for i in RSETS[2]:
        for dq in range(2):
            produce(i, dq)
    to_core.wait_recv()
    s1[...] = (rgb[k].astype(F32) + rk[...].astype(F32)).astype(BF)

    def to_plane(d, _):
        to = (z + d) % 4
        remote(s1.at[pl.ds(to * 16, 16)], rz.at[z], rg_s.at[1], rg_r.at[1], ident(x, y, to, k)).start()
        return 0

    lax.fori_loop(1, 4, to_plane, 0)
    pltpu.make_async_copy(s1.at[pl.ds(z * 16, 16)], rz.at[z], rg_r.at[1]).start()
    give(RSETS[2])
    for j in range(7):
        cols = slice(j * 512, j * 512 + 512)
        extra(j * 512, 512)[...] = dot_nt(kd_dlogit, router[cols, :]) + dot_nt(gate_dlogit, router[cols, :])
    for i in RSETS[0] + RSETS[1]:
        combine(i)
    arrived(rz, rg_r.at[1])
    arrived(rz.at[pl.ds(0, 3)], rg_s.at[1])
    s1[0:16] = jnp.sum(rz[...].astype(F32), axis=0).astype(BF)

    def to_owner(s, _):
        dx, dy, _ = offsets(s)
        tx, ty = (x + dx) % 4, (y + dy) % 4
        remote(s1.at[tx * 4 + ty], rx.at[x * 4 + y], rg_s.at[2], rg_r.at[2], ident(tx, ty, z, k)).start()
        return 0

    lax.fori_loop(1, 16, to_owner, 0)
    pltpu.make_async_copy(s1.at[x * 4 + y], rx.at[x * 4 + y], rg_r.at[2]).start()
    for i in RSETS[2]:
        combine(i)
    arrived(rx, rg_r.at[2])
    router_grad[...] = jnp.sum(rx[...].astype(F32), axis=0)[:28, :] / math.sqrt(E * T)

    for i in range(NR):
        wide = RETURN[i][1]
        arrived(back[i], part_r.at[i])
        for q in range(2):
            start = RBASE[i] + q * wide
            total = jnp.sum(back[i][q].astype(F32), axis=0) + extra(start, wide)[...]
            token_grad[:, start : start + wide] = total.astype(BF)

    for i in range(NC):
        arrived(r1[i].at[:, pl.ds(0, 7)], r1_s.at[i])
        arrived(x2[i].at[0], x2_s.at[i])
        arrived(x2[i].at[0, pl.ds(0, 15)], x2_s.at[i])
    for i in range(NR):
        arrived(yin[i].at[pl.ds(0, 31)], y_s.at[i])
        arrived(part[i].at[pl.ds(0, 7)], part_s.at[i])
    for axis in range(3):
        arrived(meta_in.at[0:7], meta_s.at[axis])
    arrived(pg_in.at[pl.ds(0, 15)], pg_s)
    arrived(bp_in.at[pl.ds(0, 7)], bp_s)
    to_core.wait_send()
    arrived(rx.at[pl.ds(0, 15)], rg_s.at[2])


def local(tokens, cotangent, router, picks, language, teacher, w_gate, w_up, w_down):
    vmem, anywhere = pl.BlockSpec(memory_space=pltpu.VMEM), pl.BlockSpec(memory_space=pl.ANY)
    buf, sem = pltpu.VMEM, pltpu.SemaphoreType.DMA
    per = lambda make, chunks=CHUNKS: tuple(buf(make(wide), BF) for _, wide in chunks)
    scratch = [
        buf((D, FF), BF), buf((D, FF), BF), buf((FF, D), BF),
        buf((2, T, D), BF),
        buf((12, T, 128), BF), buf((24, T, 128), BF),
        buf((3, 768, 256), BF), buf((3, 256, 768), BF),
        per(lambda c: (2, 8, T, c)),
        per(lambda c: (32, 48, c)), per(lambda c: (2, 16, 48, c)),
        buf((ROWS, 4 * FF), BF), buf((16, 24, D), BF),
        buf((3, ROWS, FF), F32), buf((ROWS, 2 * FF), BF),
        per(lambda c: (32, 24, c), RETURN),
        per(lambda c: (8, T, c), RETURN), per(lambda c: (2, 4, T, c), RETURN),
        buf((16, 24, 128), BF), buf((16, 24, 128), BF),
        buf((8, T, 128), BF), buf((8, T, 128), BF),
        buf((3, T, E), F32),
        buf((904, 128), F32), buf((2, 64, 32, 128), BF), buf((64, 32, 128), BF),
        buf((64, 32, 128), BF), buf((4, 16, 32, 128), BF),
        buf((16, 32, 128), BF),
        pltpu.SemaphoreType.REGULAR, sem((3,)), sem((3,)),
        sem((NC,)), sem((NC,)), sem((3,)), sem((3,)), sem((3,)), sem((3,)), sem((NC,)), sem((NC,)), sem((NR,)), sem((NR,)), sem((NR,)), sem((NR,)),
        sem, sem, sem, sem, sem((3,)), sem((3,)),
    ]
    return pl.pallas_call(
        kernel,
        out_shape=(jax.ShapeDtypeStruct((T, D), BF), jax.ShapeDtypeStruct((28, 128), F32)),
        in_specs=[anywhere, anywhere, vmem, vmem, vmem, vmem, anywhere, anywhere, anywhere, vmem, anywhere]
        + [vmem] * 4,
        out_specs=(vmem, vmem),
        scratch_shapes=scratch,
        compiler_params=pltpu.CompilerParams(
            collective_id=0, has_side_effects=True, vmem_limit_bytes=61 << 20
        ),
        cost_estimate=pl.CostEstimate(flops=15_000_000_000, bytes_accessed=24_000_000, transcendentals=400_000),
    )(tokens, cotangent, router, picks.T, language.reshape(1, T), teacher, w_gate, w_up, w_down, *tables())


def solution(mesh):
    split = P(("row", "col"), None)
    cube = P(("row", "col"), None, None)
    return jax.shard_map(
        local,
        mesh=mesh,
        in_specs=(split, split, P(), split, P(("row", "col")), P(), cube, cube, cube),
        out_specs=(split, split),
        check_vma=False,
    )
```
